1024 devices in a mesh: gx: 8 (over y, core), gy: 16 (over z_hi, x), gz: 8 (over z_lo).
Axes of the slice: x: 4, y: 4, z: 32 (z_hi: 4, z_lo: 8; z = z_hi * 8 + z_lo), core: 2. Of those that a mesh axis runs over, the one named last changes fastest.
Arguments:
- source: float32 [128, 256, 1024], P('gx', 'gy', 'gz'), may hold values from -48 to 48, as said below
- metric_xx: float32 [128, 256, 1024], P('gx', 'gy', 'gz'), may hold values from 0.004 to 0.04
- metric_yy: float32 [128, 256, 1024], P('gx', 'gy', 'gz'), may hold values from 0.004 to 0.04
- metric_zz: float32 [128, 256, 1024], P('gx', 'gy', 'gz'), may hold values from 0.004 to 0.04
- mass_term: float32 [128, 256, 1024], P('gx', 'gy', 'gz'), may hold values from 0.3 to 3
Outputs:
- solution: float32 [128, 256, 1024], P('gx', 'gy', 'gz')
- residual: float32 [128, 256, 1024], P('gx', 'gy', 'gz')
The draws below stay inside these ranges and needn't reach their ends.
Inputs may be any that keep to these rules, and one draw needn't show every extreme that they name: `source`: element-local loads; not continuous across elements.
All inputs are finite; a program needn't handle non-finite values.
Results may differ from the reference program's by a relative error of at most 0.0003.
Values sent between devices are 32-bit elements; how exact they have to be, the bound alone decides.
A program may use at most 32 MiB of HBM per device.

```python
import math
import jax
import jax.numpy as jnp
import numpy as np
from jax import lax

ITERS = 4
PX = 128
PY = 256
PZ = 1024


def draw_source(key, part):
    key = jax.random.fold_in(key, 11)
    rise = math.log(3.0)
    along_x = jnp.exp(rise * (jnp.arange(PX, dtype=jnp.float32) / PX - 0.5))
    along_y = jnp.exp(rise * (jnp.arange(PY, dtype=jnp.float32) / PY - 0.5))
    along_z = jnp.exp(rise * (jnp.arange(PZ, dtype=jnp.float32) / PZ - 0.5))
    scales = along_x[:, None, None] * along_y[None, :, None] * along_z[None, None, :]
    values = jnp.clip(jax.random.normal(key, (PX, PY, PZ), jnp.float32), -4.0, 4.0) * scales
    return jnp.clip(values, -48.0, 48.0).astype(jnp.float32)


def level_of(own_key, dims, pieces, smallest, top_value):
    def one(position, blocks):
        heights = jax.random.uniform(jax.random.fold_in(jax.random.fold_in(own_key, 6), position), (blocks,), jnp.float32, smallest / len(pieces), top_value / len(pieces))
        return jnp.repeat(jnp.exp(heights), dims[position] // blocks).reshape((-1,) + (1,) * (len(dims) - position - 1))

    gain = one(*pieces[0])
    for cut in pieces[1:]:
        gain = gain * one(*cut)
    return gain


def setup_inputs(seed: int = 0) -> dict:
    streams_of = jax.random.split(jax.random.key(seed), 6)
    return {
        "source": draw_source(jax.random.fold_in(streams_of[5], 71), 0),
        "metric_xx": jnp.clip(jnp.exp(math.log(0.04) - 2.30258502 * jax.random.uniform(streams_of[1], (PX, PY, PZ), jnp.float32) ** level_of(streams_of[1], (PX, PY, PZ), ((0, 8), (1, 16), (2, 8)), -0.2, 0.2)), 0.004, 0.04),
        "metric_yy": jnp.clip(jnp.exp(math.log(0.04) - 2.30258502 * jax.random.uniform(streams_of[2], (PX, PY, PZ), jnp.float32) ** level_of(streams_of[2], (PX, PY, PZ), ((0, 8), (1, 16), (2, 8)), -0.2, 0.2)), 0.004, 0.04),
        "metric_zz": jnp.clip(jnp.exp(math.log(0.04) - 2.30258502 * jax.random.uniform(streams_of[3], (PX, PY, PZ), jnp.float32) ** level_of(streams_of[3], (PX, PY, PZ), ((0, 8), (1, 16), (2, 8)), -0.2, 0.2)), 0.004, 0.04),
        "mass_term": jnp.clip(jnp.exp(math.log(3.0) - 2.3025851 * jax.random.uniform(streams_of[4], (PX, PY, PZ), jnp.float32) ** level_of(streams_of[4], (PX, PY, PZ), ((0, 8), (1, 16), (2, 8)), -0.2, 0.2)), 0.3, 3.0),
    }


def derivative_table():
    points = np.array([-1.0, -0.8717401485096066, -0.5917001814331423, -0.2092992179024789,
                       0.2092992179024789, 0.5917001814331423, 0.8717401485096066, 1.0])
    weights_c = np.array([np.prod([points[row_index] - points[col_index] for col_index in range(8) if col_index != row_index]) for row_index in range(8)])
    table = np.zeros((8, 8))
    for row_index in range(8):
        for col_index in range(8):
            if row_index != col_index:
                table[row_index, col_index] = weights_c[row_index] / (weights_c[col_index] * (points[row_index] - points[col_index]))
        table[row_index, row_index] = -np.sum(table[row_index])
    return jnp.asarray(table, jnp.float32)


def apply_along(field, matrix, which_dim):
    extent_x, extent_y, extent_z = field.shape
    if which_dim == 0:
        blocks = field.reshape(extent_x // 8, 8, extent_y, extent_z)
        result = jnp.einsum('ki,aibc->akbc', matrix, blocks, precision=lax.Precision.HIGHEST)
    elif which_dim == 1:
        blocks = field.reshape(extent_x, extent_y // 8, 8, extent_z)
        result = jnp.einsum('ki,abic->abkc', matrix, blocks, precision=lax.Precision.HIGHEST)
    else:
        blocks = field.reshape(extent_x, extent_y, extent_z // 8, 8)
        result = jnp.einsum('ki,abci->abck', matrix, blocks, precision=lax.Precision.HIGHEST)
    return result.reshape(field.shape)


def local_apply(field, derivative, metric_xx, metric_yy, metric_zz, mass_term):
    total = mass_term * field
    for which_dim, factor in ((0, metric_xx), (1, metric_yy), (2, metric_zz)):
        slope = apply_along(field, derivative, which_dim)
        total = total + apply_along(factor * slope, derivative.T, which_dim)
    return total


def local_diagonal(derivative, metric_xx, metric_yy, metric_zz, mass_term):
    squared = (derivative * derivative).T
    total = mass_term
    for which_dim, factor in ((0, metric_xx), (1, metric_yy), (2, metric_zz)):
        total = total + apply_along(factor, squared, which_dim)
    return total


def pair_sum(padded, which_dim):
    extent = padded.shape[which_dim] - 2
    middle = lax.slice_in_dim(padded, 1, extent + 1, axis=which_dim)
    following = lax.slice_in_dim(padded, 2, extent + 2, axis=which_dim)
    previous = lax.slice_in_dim(padded, 0, extent, axis=which_dim)
    within = lax.iota(jnp.int32, extent) % 8
    layout = [1, 1, 1]
    layout[which_dim] = extent
    closing = (within == 7).reshape(layout)
    opening = (within == 0).reshape(layout)
    return middle + jnp.where(closing, following, 0.0) + jnp.where(opening, previous, 0.0)


def copies(extent, offset, total):
    slots = offset + lax.iota(jnp.int32, extent)
    more = jnp.where((slots % 8 == 7) & (slots != total - 1), 1.0, 0.0)
    more = more + jnp.where((slots % 8 == 0) & (slots != 0), 1.0, 0.0)
    return (1.0 + more).astype(jnp.float32)


def assemble(field):
    for which_dim in range(3):
        widths = [(0, 0), (0, 0), (0, 0)]
        widths[which_dim] = (1, 1)
        field = pair_sum(jnp.pad(field, widths), which_dim)
    return field


def reference(source, metric_xx, metric_yy, metric_zz, mass_term):
    derivative = derivative_table()
    extent_x, extent_y, extent_z = source.shape
    weights = 1.0 / (copies(extent_x, 0, extent_x)[:, None, None] * copies(extent_y, 0, extent_y)[None, :, None] * copies(extent_z, 0, extent_z)[None, None, :])
    jacobi = 1.0 / assemble(local_diagonal(derivative, metric_xx, metric_yy, metric_zz, mass_term))

    def operator(field):
        return assemble(local_apply(field, derivative, metric_xx, metric_yy, metric_zz, mass_term))

    solution = jnp.zeros_like(source)
    residual = assemble(source)
    smoothed = jacobi * residual
    image = operator(smoothed)
    search = jnp.zeros_like(source)
    search_img = jnp.zeros_like(source)
    search_pre = jnp.zeros_like(source)
    search_op = jnp.zeros_like(source)
    gamma_old = jnp.float32(1.0)
    alpha_old = jnp.float32(1.0)
    for iteration in range(ITERS):
        gamma_now = jnp.sum(weights * residual * smoothed)
        delta_now = jnp.sum(weights * image * smoothed)
        image_pre = jacobi * image
        image_op = operator(image_pre)
        if iteration == 0:
            beta_now = jnp.float32(0.0) * gamma_now
            alpha_now = gamma_now / delta_now
        else:
            beta_now = gamma_now / gamma_old
            alpha_now = gamma_now / (delta_now - beta_now * gamma_now / alpha_old)
        search_op = image_op + beta_now * search_op
        search_pre = image_pre + beta_now * search_pre
        search_img = image + beta_now * search_img
        search = smoothed + beta_now * search
        solution = solution + alpha_now * search
        residual = residual - alpha_now * search_img
        smoothed = smoothed - alpha_now * search_pre
        image = image - alpha_now * search_op
        gamma_old = gamma_now
        alpha_old = alpha_now
    return solution, residual
```

```python
import itertools

import jax
import jax.numpy as jnp
import numpy as np
from jax import lax
from jax.experimental import pallas as pl
from jax.experimental.pallas import tpu as pltpu
from jax.sharding import PartitionSpec as P

MESH = pl.DeviceIdType.MESH
ITERS = 4
CENTRE, HALF = 1.2, 1.1
AXES = ("gx", "gy", "gz")

NEAR = sorted(
    (o for o in itertools.product((-1, 0, 1), repeat=3) if o != (0, 0, 0)),
    key=lambda o: (o[1] == 0, -abs(o[0]) - abs(o[2])),
)


def derivative_table():
    points = np.array(
        [
            -1.0,
            -0.8717401485096066,
            -0.5917001814331423,
            -0.2092992179024789,
            0.2092992179024789,
            0.5917001814331423,
            0.8717401485096066,
            1.0,
        ]
    )
    gaps = points[:, None] - points[None, :] + np.eye(8)
    weights_c = np.prod(gaps, axis=1)
    table = weights_c[:, None] / (weights_c[None, :] * gaps)
    table = table - np.diag(np.diag(table))
    return table - np.diag(table.sum(axis=1))


TABLE = derivative_table()


def sublane_factors(matrix):
    k = np.arange(8)
    rows = np.stack([matrix[k, (k + s) % 8] for s in range(8)])
    return np.repeat(rows[:, :, None], 128, axis=2)


def constants():
    square = (TABLE * TABLE).T
    mats = [np.kron(np.eye(16), m.T) for m in (TABLE, TABLE.T, square)]
    facs = [sublane_factors(m) for m in (TABLE, TABLE.T, square)]
    return np.stack(mats).astype(np.float32), np.stack(facs).astype(np.float32)


def along_x(field, matrix):
    out = [None] * 16
    for base in (0, 8):
        even = [field[base + i] + field[base + 7 - i] for i in range(4)]
        odd = [field[base + i] - field[base + 7 - i] for i in range(4)]
        for k in range(4):
            e = sum(float(0.5 * (matrix[k, i] + matrix[k, 7 - i])) * even[i] for i in range(4))
            o = sum(float(0.5 * (matrix[k, i] - matrix[k, 7 - i])) * odd[i] for i in range(4))
            out[base + k] = o + e
            out[base + 7 - k] = o - e
    return out


def along_x_plain(field, matrix):
    return [
        sum(float(matrix[k % 8, i]) * field[k // 8 * 8 + i] for i in range(8)) for k in range(16)
    ]


def along_y(field, facs):
    total = field * facs[0][None]
    for s in range(1, 8):
        total = total + pltpu.roll(field, 8 - s, 1) * facs[s][None]
    return total


def along_z(field, mat):
    flat = field.reshape(256, 128)
    return jnp.dot(flat, mat, precision=lax.Precision.HIGHEST, preferred_element_type=jnp.float32)


def slabs(field):
    return [field[i] for i in range(16)]


def kernel(
    dims, xwidth,
    src_ref, mx_ref, my_ref, mz_ref, mass_ref, mats_ref, facs_ref,
    sol_ref, res_ref,
    jac, T, L, V, Z, A, YS, PS, XF, YF, ZF, XZ, RB, acc, row_a, row_b, buf_a, buf_b,
    ssem, rsem, ssem_a, rsem_a, ssem_b, rsem_b,
):
    nx, ny, nz = dims
    ix, iy, iz = (lax.axis_index(a) for a in AXES)
    here = {0: (ix, nx), 1: (iy, ny), 2: (iz, nz)}

    def exists(o):
        ok = None
        for d in range(3):
            at, n = here[d]
            c = at > 0 if o[d] < 0 else at < n - 1 if o[d] > 0 else None
            ok = c if ok is None else ok if c is None else jnp.logical_and(ok, c)
        return ok

    def dev(o):
        return (ix + o[0], iy + o[1], iz + o[2])

    depth = ny // xwidth
    plane, ring = nx * xwidth, depth * nz
    my_a = ix * xwidth + lax.rem(iy, xwidth)
    my_b = (iy // xwidth) * nz + iz

    def dev_a(k):
        to = lax.rem(my_a + k, plane)
        return (to // xwidth, (iy // xwidth) * xwidth + lax.rem(to, xwidth), iz)

    def dev_b(k):
        to = lax.rem(my_b + k, ring)
        return (ix, (to // nz) * xwidth + lax.rem(iy, xwidth), lax.rem(to, nz))

    def far_first(i, n):
        half = (i + 1) // 2
        return n // 2 + jnp.where(lax.rem(i, 2) == 1, half, -half)

    for ref in (XF, YF, ZF, XZ, RB):
        ref[...] = jnp.zeros_like(ref)
    barrier = pltpu.get_barrier_semaphore()

    def greet(group, n):
        def body(i, c):
            pl.semaphore_signal(barrier, inc=1, device_id=group(far_first(i, n)), device_id_type=MESH)
            return c
        lax.fori_loop(0, n - 1, body, 0)

    greet(dev_b, ring)
    for o in NEAR:
        @pl.when(exists(o))
        def _(o=o):
            pl.semaphore_signal(barrier, inc=1, device_id=dev(o), device_id_type=MESH)
    greet(dev_a, plane)
    sides = [1 + (at > 0).astype(jnp.int32) + (at < n - 1).astype(jnp.int32) for at, n in here.values()]
    n_near = sides[0] * sides[1] * sides[2] - 1

    lane = lax.broadcasted_iota(jnp.int32, (8, 128), 1)
    sub = lax.broadcasted_iota(jnp.int32, (8, 128), 0)
    within = lax.rem(lane, 8)
    close = jnp.where((within == 7) & (lane != 127), 1.0, 0.0)[None]
    opens = jnp.where((within == 0) & (lane != 0), 1.0, 0.0)[None]
    even = lax.rem(lane, 2) == 0
    low = lax.rem(lane, 4) < 2
    ends_y = (low & (sub == 0)) | (jnp.logical_not(low) & (sub == 7))
    ends_z = (lane == 0) | (lane == 127)

    def prepare(s, f, raw):
        v = raw.reshape(32, 8, 128)
        v = v + pltpu.roll(v, 127, 2) * close + pltpu.roll(v, 1, 2) * opens
        t = T.at[s, f]
        t[...] = v.reshape(16, 16, 128)
        both = t[7] + t[8]
        t[7] = both
        t[8] = both
        both = t[:, 7, :] + t[:, 8, :]
        t[:, 7, :] = both
        t[:, 8, :] = both
        YS[s, f, 0] = t[:, 0, :]
        YS[s, f, 1] = t[:, 15, :]
        packed = jnp.zeros((8, 128), jnp.float32)
        for i in range(32):
            tile = t[i // 2, pl.ds(8 * (i % 2), 8), :]
            packed = jnp.where(lane // 2 == i, pltpu.roll(tile, 2 * i + 1, 1), packed)
        PS[s, f] = packed

    def end(d):
        return 0 if d < 0 else 1

    def copies(s, fields):
        fs = pl.ds(0, fields)
        for n, o in enumerate(NEAR):
            dx, dy, dz = o
            ex, ey, ez = end(-dx), end(-dy), end(-dz)
            edge = pl.ds(7 * end(dy), 1)
            if dz == 0:
                if dy == 0:
                    src, dst = T.at[s, fs, 15 * end(dx)], XF.at[s, fs, ex]
                elif dx == 0:
                    src, dst = YS.at[s, fs, end(dy)], YF.at[s, fs, ey]
                else:
                    src = YS.at[s, fs, end(dy), pl.ds(15 * end(dx), 1)]
                    dst = RB.at[s, fs, pl.ds(2 * ex + ey, 1)]
            elif dy == 0:
                src = PS.at[s, fs]
                dst = ZF.at[s, fs, ez] if dx == 0 else XZ.at[s, fs, 2 * ex + ez]
            else:
                src = PS.at[s, fs, edge]
                slot = 4 + 2 * ey + ez if dx == 0 else 8 + 4 * ex + 2 * ey + ez
                dst = RB.at[s, fs, pl.ds(slot, 1)]
            yield o, pltpu.make_async_remote_copy(
                src_ref=src, dst_ref=dst, send_sem=ssem.at[s, n], recv_sem=rsem.at[s, n],
                device_id=dev(o), device_id_type=MESH,
            )

    def send(s, fields):
        for o, copy in copies(s, fields):
            pl.when(exists(o))(copy.start)

    def receive(s, fields):
        order = {o: n for n, o in enumerate(NEAR)}
        for o, copy in copies(s, fields):
            back = tuple(-d for d in o)
            pl.when(exists(back))(copy.wait_recv)

    def sent(s, fields):
        for o, copy in copies(s, fields):
            pl.when(exists(o))(copy.wait_send)

    def merge(minus, plus):
        return jnp.where(even, pltpu.roll(plus, 127, 1), pltpu.roll(minus, 1, 1))

    def finish(s, f, out):
        rb = RB.at[s, f]

        def line(k):
            return jnp.broadcast_to(rb[pl.ds(k, 1), :], (8, 128))

        def with_y(m, first):
            minus = merge(line(first), line(first + 1))
            plus = merge(line(first + 2), line(first + 3))
            c = jnp.where(low, pltpu.roll(minus, 126, 1), pltpu.roll(plus, 2, 1))
            return m + jnp.where(ends_y, c, 0.0)

        m = with_y(merge(ZF[s, f, 0], ZF[s, f, 1]), 4)
        m_minus = with_y(merge(XZ[s, f, 0], XZ[s, f, 1]), 8)
        m_plus = with_y(merge(XZ[s, f, 2], XZ[s, f, 3]), 12)
        m = m + jnp.where(lane < 4, pltpu.roll(m_minus, 68, 1), 0.0)
        m = m + jnp.where((lane >= 60) & (lane < 64), pltpu.roll(m_plus, 60, 1), 0.0)
        for i in range(32):
            at = (i // 2, pl.ds(8 * (i % 2), 8), slice(None))
            part = jnp.where(ends_z, pltpu.roll(m, 127 - 2 * i, 1), 0.0)
            out[at] = T[(s, f) + at] + part
        out[:, 0, :] = out[:, 0, :] + YF[s, f, 0]
        out[:, 15, :] = out[:, 15, :] + YF[s, f, 1]
        for e in (0, 1):
            out[15 * e] = out[15 * e] + XF[s, f, e]
            for g in (0, 1):
                r = pl.ds(15 * g, 1)
                out[15 * e, r, :] = out[15 * e, r, :] + rb[pl.ds(2 * e + g, 1), :]

    def local(v):
        total = mass_ref[...] * v
        slope = along_x(slabs(v), TABLE)
        slope = [mx_ref[i] * slope[i] for i in range(16)]
        total = total + jnp.stack(along_x(slope, TABLE.T))
        v3 = v.reshape(32, 8, 128)
        slope = my_ref[...].reshape(32, 8, 128) * along_y(v3, facs_ref[0])
        total = total + along_y(slope, facs_ref[1]).reshape(16, 16, 128)
        slope = mz_ref[...].reshape(256, 128) * along_z(v, mats_ref[0])
        return total + along_z(slope, mats_ref[1]).reshape(16, 16, 128)

    def product(slot, a, b):
        acc[slot] = jnp.sum((a * b).reshape(32, 8, 128), axis=0)

    def products(j, count):
        for i in range(count):
            product(4 * j + i, L[...], V[i])
        product(16 + j, src_ref[...], V[j])

    diag = mass_ref[...] + jnp.stack(along_x_plain(slabs(mx_ref[...]), (TABLE * TABLE).T))
    diag = diag + along_y(my_ref[...].reshape(32, 8, 128), facs_ref[2]).reshape(16, 16, 128)
    diag = diag + along_z(mz_ref[...], mats_ref[2]).reshape(16, 16, 128)
    prepare(0, 0, src_ref[...])
    prepare(0, 1, diag)
    pl.semaphore_wait(barrier, n_near + (plane - 1) + (ring - 1))
    send(0, 2)
    V[...] = jnp.zeros_like(V)
    acc[...] = jnp.zeros_like(acc)
    Z[0] = jnp.zeros((16, 16, 128), jnp.float32)
    receive(0, 2)
    finish(0, 0, Z.at[1])
    finish(0, 1, jac)
    jac[...] = 1.0 / jac[...]
    V[0] = jac[...] * Z[1]

    def step(j, c):
        L[...] = local(V[j])
        prepare(j + 1, 0, L[...])
        send(j + 1, 1)
        products(j, ITERS)
        receive(j + 1, 1)
        finish(j + 1, 0, A.at[j])
        first = j == 0
        gain = jnp.where(first, 1.0 / HALF, 2.0 / HALF)
        z = gain * (A[j] - CENTRE * Z[j + 1]) - jnp.where(first, 0.0, 1.0) * Z[j]
        Z[j + 2] = z
        V[j + 1] = jac[...] * z
        return c

    lax.fori_loop(0, ITERS - 1, step, 0)

    last = ITERS - 1
    L[...] = local(V[last])
    products(last, ITERS)
    sums = jnp.sum(acc[...], axis=1)
    sums = jnp.sum(sums, axis=1, keepdims=True)
    pick = lax.broadcasted_iota(jnp.int32, (24, 128), 0) == lax.broadcasted_iota(jnp.int32, (24, 128), 1)

    def share(row, buf, me, group, n, ss, rs, values):
        row[...] = values
        buf[me] = values

        def copy(i):
            k = far_first(i, n)
            return pltpu.make_async_remote_copy(
                src_ref=row, dst_ref=buf.at[me], send_sem=ss.at[k], recv_sem=rs.at[k],
                device_id=group(k), device_id_type=MESH,
            )

        def begin(i, c):
            copy(i).start()
            return c

        def arrive(i, c):
            copy(i).wait_recv()
            return c

        def left(i, c):
            copy(i).wait_send()
            return c

        lax.fori_loop(0, n - 1, begin, 0)
        return lambda: lax.fori_loop(0, n - 1, arrive, 0), lambda: lax.fori_loop(0, n - 1, left, 0)

    values = jnp.sum(jnp.where(pick, sums, 0.0), axis=0, keepdims=True)
    arrive_a, left_a = share(row_a, buf_a, my_a, dev_a, plane, ssem_a, rsem_a, values)
    prepare(ITERS, 0, L[...])
    send(ITERS, 1)
    arrive_a()
    values = jnp.sum(buf_a[...], axis=0)
    arrive_b, left_b = share(row_b, buf_b, my_b, dev_b, ring, ssem_b, rsem_b, values)
    receive(ITERS, 1)
    finish(ITERS, 0, A.at[last])
    arrive_b()
    values = jnp.broadcast_to(jnp.sum(buf_b[...], axis=0), (8, 128))

    def value(k):
        return jnp.sum(jnp.where(lane == k, values, 0.0), axis=1, keepdims=True)

    H = [[value(4 * max(i, j) + min(i, j)) for j in range(ITERS)] for i in range(ITERS)]
    g = [value(16 + i) for i in range(ITERS)]
    for k in range(ITERS):
        inv = 1.0 / H[k][k]
        for i in range(k + 1, ITERS):
            f = H[i][k] * inv
            for j in range(k + 1, ITERS):
                H[i][j] = H[i][j] - f * H[k][j]
            g[i] = g[i] - f * g[k]
    y = [None] * ITERS
    for k in reversed(range(ITERS)):
        s = g[k]
        for j in range(k + 1, ITERS):
            s = s - H[k][j] * y[j]
        y[k] = s / H[k][k]

    wide = [jnp.broadcast_to(c, (8, 128))[None] for c in y]
    total = wide[0] * V[0].reshape(32, 8, 128)
    rest = Z[1].reshape(32, 8, 128) - wide[0] * A[0].reshape(32, 8, 128)
    for j in range(1, ITERS):
        total = total + wide[j] * V[j].reshape(32, 8, 128)
        rest = rest - wide[j] * A[j].reshape(32, 8, 128)
    sol_ref[...] = total.reshape(16, 16, 128)
    res_ref[...] = rest.reshape(16, 16, 128)

    sent(0, 2)

    def settle(s, c):
        sent(s, 1)
        return c

    lax.fori_loop(1, ITERS + 1, settle, 0)
    left_a()
    left_b()


def solution(mesh):
    dims = tuple(mesh.shape[a] for a in AXES)
    xwidth = min(4, dims[1] // 2)
    plane, ring = dims[0] * xwidth, dims[1] // xwidth * dims[2]
    near = len(NEAR)
    steps = ITERS + 1
    f32 = jnp.float32
    block = (16, 16, 128)
    vmem = pl.BlockSpec(memory_space=pltpu.VMEM)
    dma = pltpu.SemaphoreType.DMA

    def body(*args):
        def run(*refs):
            kernel(dims, xwidth, *refs)

        mats, facs = constants()
        return pl.pallas_call(
            run,
            out_shape=[jax.ShapeDtypeStruct(block, f32)] * 2,
            in_specs=[vmem] * 7,
            out_specs=[vmem] * 2,
            scratch_shapes=[
                pltpu.VMEM(block, f32),
                pltpu.VMEM((steps, 2) + block, f32),
                pltpu.VMEM(block, f32),
                pltpu.VMEM((ITERS,) + block, f32),
                pltpu.VMEM((ITERS + 1,) + block, f32),
                pltpu.VMEM((ITERS,) + block, f32),
                pltpu.VMEM((steps, 2, 2, 16, 128), f32),
                pltpu.VMEM((steps, 2, 8, 128), f32),
                pltpu.VMEM((steps, 2, 2, 16, 128), f32),
                pltpu.VMEM((steps, 2, 2, 16, 128), f32),
                pltpu.VMEM((steps, 2, 2, 8, 128), f32),
                pltpu.VMEM((steps, 2, 4, 8, 128), f32),
                pltpu.VMEM((steps, 2, 16, 128), f32),
                pltpu.VMEM((24, 8, 128), f32),
                pltpu.VMEM((1, 128), f32),
                pltpu.VMEM((1, 128), f32),
                pltpu.VMEM((plane, 1, 128), f32),
                pltpu.VMEM((ring, 1, 128), f32),
                dma((steps, near)),
                dma((steps, near)),
                dma((plane,)),
                dma((plane,)),
                dma((ring,)),
                dma((ring,)),
            ],
            compiler_params=pltpu.CompilerParams(
                collective_id=0, has_side_effects=True, vmem_limit_bytes=32 * 1024 * 1024
            ),
        )(*args, jnp.asarray(mats), jnp.asarray(facs))

    spec = P(*AXES)
    return jax.shard_map(
        body, mesh=mesh, in_specs=(spec,) * 5, out_specs=(spec,) * 2, check_vma=False
    )
```

```python
import itertools

import jax
import jax.numpy as jnp
import numpy as np
from jax import lax
from jax.experimental import pallas as pl
from jax.experimental.pallas import tpu as pltpu
from jax.sharding import PartitionSpec as P

MESH = pl.DeviceIdType.MESH
ITERS = 4
CENTRE, HALF = 1.2, 1.1
AXES = ("gx", "gy", "gz")

NEAR = sorted(
    (o for o in itertools.product((-1, 0, 1), repeat=3) if o != (0, 0, 0)),
    key=lambda o: (o[1] == 0, -abs(o[0]) - abs(o[2])),
)


def derivative_table():
    points = np.array(
        [
            -1.0,
            -0.8717401485096066,
            -0.5917001814331423,
            -0.2092992179024789,
            0.2092992179024789,
            0.5917001814331423,
            0.8717401485096066,
            1.0,
        ]
    )
    gaps = points[:, None] - points[None, :] + np.eye(8)
    weights_c = np.prod(gaps, axis=1)
    table = weights_c[:, None] / (weights_c[None, :] * gaps)
    table = table - np.diag(np.diag(table))
    return table - np.diag(table.sum(axis=1))


TABLE = derivative_table()


def sublane_factors(matrix):
    k = np.arange(8)
    rows = np.stack([matrix[k, (k + s) % 8] for s in range(8)])
    return np.repeat(rows[:, :, None], 128, axis=2)


def constants():
    square = (TABLE * TABLE).T
    mats = [np.kron(np.eye(16), m.T) for m in (TABLE, TABLE.T, square)]
    facs = [sublane_factors(m) for m in (TABLE, TABLE.T, square)]
    return np.stack(mats).astype(np.float32), np.stack(facs).astype(np.float32)


def along_x(field, matrix):
    out = [None] * 16
    for base in (0, 8):
        even = [field[base + i] + field[base + 7 - i] for i in range(4)]
        odd = [field[base + i] - field[base + 7 - i] for i in range(4)]
        for k in range(4):
            e = sum(float(0.5 * (matrix[k, i] + matrix[k, 7 - i])) * even[i] for i in range(4))
            o = sum(float(0.5 * (matrix[k, i] - matrix[k, 7 - i])) * odd[i] for i in range(4))
            out[base + k] = o + e
            out[base + 7 - k] = o - e
    return out


def along_x_plain(field, matrix):
    return [
        sum(float(matrix[k % 8, i]) * field[k // 8 * 8 + i] for i in range(8)) for k in range(16)
    ]


def along_y(field, facs):
    total = field * facs[0][None]
    for s in range(1, 8):
        total = total + pltpu.roll(field, 8 - s, 1) * facs[s][None]
    return total


def along_z(field, mat):
    flat = field.reshape(256, 128)
    return jnp.dot(flat, mat, precision=lax.Precision.HIGHEST, preferred_element_type=jnp.float32)


def slabs(field):
    return [field[i] for i in range(16)]


def kernel(
    dims, xwidth,
    src_hbm, mx_hbm, my_hbm, mz_hbm, mass_hbm, mats_hbm, facs_hbm,
    sol_ref, res_ref,
    src_ref, mx_ref, my_ref, mz_ref, mass_ref, mats_ref, facs_ref,
    jac, T, L, V, Z, A, YS, PS, XF, YF, ZF, XZ, RB, acc, count, row_a, row_b, buf_a, buf_b,
    ssem, rsem, ssem_a, rsem_a, ssem_b, rsem_b, lsem,
):
    nx, ny, nz = dims
    ix, iy, iz = (lax.axis_index(a) for a in AXES)
    here = {0: (ix, nx), 1: (iy, ny), 2: (iz, nz)}

    def exists(o):
        ok = None
        for d in range(3):
            at, n = here[d]
            c = at > 0 if o[d] < 0 else at < n - 1 if o[d] > 0 else None
            ok = c if ok is None else ok if c is None else jnp.logical_and(ok, c)
        return ok

    def dev(o):
        return (ix + o[0], iy + o[1], iz + o[2])

    depth = ny // xwidth
    plane, ring = nx * xwidth, depth * nz
    col, high = lax.rem(iy, xwidth), iy // xwidth
    my_a = ix * xwidth + col
    my_b = high * nz + iz

    def carry(at, by, n):
        to = at + by
        over = to >= n
        return jnp.where(over, to - n, to), over.astype(jnp.int32)

    def dev_a(k):
        x, up = carry(col, k % xwidth, xwidth)
        return carry(ix, k // xwidth + up, nx)[0], high * xwidth + x, iz

    def dev_b(k):
        z, up = carry(iz, k % nz, nz)
        return ix, carry(high, k // nz + up, depth)[0] * xwidth + col, z

    def far_first(n):
        return sorted(range(1, n), key=lambda k: abs(2 * k - n))

    loads = [
        pltpu.make_async_copy(a, b, lsem.at[i])
        for i, (a, b) in enumerate(
            (
                (src_hbm, src_ref),
                (mats_hbm, mats_ref),
                (facs_hbm, facs_ref),
                (mx_hbm, mx_ref),
                (my_hbm, my_ref),
                (mz_hbm, mz_ref),
                (mass_hbm, mass_ref),
            )
        )
    ]
    for load in loads:
        load.start()
    for ref in (XF, YF, ZF, XZ, RB):
        ref[0] = jnp.zeros(ref.shape[1:], jnp.float32)
    barrier = pltpu.get_barrier_semaphore()

    def greet(group, n):
        for k in far_first(n):
            pl.semaphore_signal(barrier, inc=1, device_id=group(k), device_id_type=MESH)

    greet(dev_b, ring)
    for o in NEAR:
        @pl.when(exists(o))
        def _(o=o):
            pl.semaphore_signal(barrier, inc=1, device_id=dev(o), device_id_type=MESH)
    greet(dev_a, plane)
    sides = [1 + (at > 0).astype(jnp.int32) + (at < n - 1).astype(jnp.int32) for at, n in here.values()]
    n_near = sides[0] * sides[1] * sides[2] - 1

    lane = lax.broadcasted_iota(jnp.int32, (8, 128), 1)
    sub = lax.broadcasted_iota(jnp.int32, (8, 128), 0)
    within = lax.rem(lane, 8)
    close = jnp.where((within == 7) & (lane != 127), 1.0, 0.0)[None]
    opens = jnp.where((within == 0) & (lane != 0), 1.0, 0.0)[None]
    even = lax.rem(lane, 2) == 0
    low = lax.rem(lane, 4) < 2
    ends_y = (low & (sub == 0)) | (jnp.logical_not(low) & (sub == 7))
    ends_z = (lane == 0) | (lane == 127)

    def prepare(s, f, raw):
        v = raw.reshape(32, 8, 128)
        v = v + pltpu.roll(v, 127, 2) * close + pltpu.roll(v, 1, 2) * opens
        t = T.at[s, f]
        t[...] = v.reshape(16, 16, 128)
        both = t[7] + t[8]
        t[7] = both
        t[8] = both
        both = t[:, 7, :] + t[:, 8, :]
        t[:, 7, :] = both
        t[:, 8, :] = both
        YS[s, f, 0] = t[:, 0, :]
        YS[s, f, 1] = t[:, 15, :]
        packed = jnp.zeros((8, 128), jnp.float32)
        for i in range(32):
            tile = t[i // 2, pl.ds(8 * (i % 2), 8), :]
            packed = jnp.where(lane // 2 == i, pltpu.roll(tile, 2 * i + 1, 1), packed)
        PS[s, f] = packed

    def end(d):
        return 0 if d < 0 else 1

    def copies(s, fields):
        fs = pl.ds(0, fields)
        for o in NEAR:
            dx, dy, dz = o
            ex, ey, ez = end(-dx), end(-dy), end(-dz)
            edge = pl.ds(7 * end(dy), 1)
            if dz == 0:
                if dy == 0:
                    src, dst = T.at[s, fs, 15 * end(dx)], XF.at[s, fs, ex]
                elif dx == 0:
                    src, dst = YS.at[s, fs, end(dy)], YF.at[s, fs, ey]
                else:
                    src = YS.at[s, fs, end(dy), pl.ds(15 * end(dx), 1)]
                    dst = RB.at[s, fs, pl.ds(2 * ex + ey, 1)]
            elif dy == 0:
                src = PS.at[s, fs]
                dst = ZF.at[s, fs, ez] if dx == 0 else XZ.at[s, fs, 2 * ex + ez]
            else:
                src = PS.at[s, fs, edge]
                slot = 4 + 2 * ey + ez if dx == 0 else 8 + 4 * ex + 2 * ey + ez
                dst = RB.at[s, fs, pl.ds(slot, 1)]
            yield o, pltpu.make_async_remote_copy(
                src_ref=src, dst_ref=dst, send_sem=ssem.at[s], recv_sem=rsem.at[s],
                device_id=dev(o), device_id_type=MESH,
            )

    def send(s, fields):
        for o, copy in copies(s, fields):
            pl.when(exists(o))(copy.start)

    def wait_all(sem, fields):
        for cx, cy, cz in itertools.product((1, 2), repeat=3):
            rows = 16 * (cx + cy) + 8 * cz + cx * cy + 8 * cx * cz + cy * cz * (1 + cx)
            here = (sides[0] == cx + 1) & (sides[1] == cy + 1) & (sides[2] == cz + 1)

            @pl.when(here)
            def _(rows=rows):
                whole = count.at[pl.ds(0, rows * fields)]
                pltpu.make_async_copy(whole, whole, sem).wait()

    def receive(s, fields):
        wait_all(rsem.at[s], fields)

    def sent(s, fields):
        wait_all(ssem.at[s], fields)

    def merge(minus, plus):
        return jnp.where(even, pltpu.roll(plus, 127, 1), pltpu.roll(minus, 1, 1))

    def finish(s, f, out):
        rb = RB.at[s, f]

        def line(k):
            return jnp.broadcast_to(rb[pl.ds(k, 1), :], (8, 128))

        def with_y(m, first):
            minus = merge(line(first), line(first + 1))
            plus = merge(line(first + 2), line(first + 3))
            c = jnp.where(low, pltpu.roll(minus, 126, 1), pltpu.roll(plus, 2, 1))
            return m + jnp.where(ends_y, c, 0.0)

        m = with_y(merge(ZF[s, f, 0], ZF[s, f, 1]), 4)
        m_minus = with_y(merge(XZ[s, f, 0], XZ[s, f, 1]), 8)
        m_plus = with_y(merge(XZ[s, f, 2], XZ[s, f, 3]), 12)
        m = m + jnp.where(lane < 4, pltpu.roll(m_minus, 68, 1), 0.0)
        m = m + jnp.where((lane >= 60) & (lane < 64), pltpu.roll(m_plus, 60, 1), 0.0)
        for i in range(32):
            at = (i // 2, pl.ds(8 * (i % 2), 8), slice(None))
            part = jnp.where(ends_z, pltpu.roll(m, 127 - 2 * i, 1), 0.0)
            out[at] = T[(s, f) + at] + part
        out[:, 0, :] = out[:, 0, :] + YF[s, f, 0]
        out[:, 15, :] = out[:, 15, :] + YF[s, f, 1]
        for e in (0, 1):
            out[15 * e] = out[15 * e] + XF[s, f, e]
            for g in (0, 1):
                r = pl.ds(15 * g, 1)
                out[15 * e, r, :] = out[15 * e, r, :] + rb[pl.ds(2 * e + g, 1), :]

    def local(v):
        total = mass_ref[...] * v
        slope = along_x(slabs(v), TABLE)
        slope = [mx_ref[i] * slope[i] for i in range(16)]
        total = total + jnp.stack(along_x(slope, TABLE.T))
        v3 = v.reshape(32, 8, 128)
        slope = my_ref[...].reshape(32, 8, 128) * along_y(v3, facs_ref[0])
        total = total + along_y(slope, facs_ref[1]).reshape(16, 16, 128)
        slope = mz_ref[...].reshape(256, 128) * along_z(v, mats_ref[0])
        return total + along_z(slope, mats_ref[1]).reshape(16, 16, 128)

    def product(slot, a, b):
        acc[slot] = jnp.sum((a * b).reshape(32, 8, 128), axis=0)

    def products(j, upto):
        for i in range(upto):
            product(4 * j + i, L[...], V[i])
        product(16 + j, src_ref[...], V[j])

    for ref in (XF, YF, ZF, XZ, RB):
        ref[1:] = jnp.zeros((ITERS,) + ref.shape[1:], jnp.float32)
    V[...] = jnp.zeros_like(V)
    acc[...] = jnp.zeros_like(acc)
    Z[0] = jnp.zeros((16, 16, 128), jnp.float32)
    loads[0].wait()
    prepare(0, 0, src_ref[...])
    for load in loads[1:]:
        load.wait()
    diag = mass_ref[...] + jnp.stack(along_x_plain(slabs(mx_ref[...]), (TABLE * TABLE).T))
    diag = diag + along_y(my_ref[...].reshape(32, 8, 128), facs_ref[2]).reshape(16, 16, 128)
    diag = diag + along_z(mz_ref[...], mats_ref[2]).reshape(16, 16, 128)
    prepare(0, 1, diag)
    pl.semaphore_wait(barrier, n_near + (plane - 1) + (ring - 1))
    send(0, 2)
    receive(0, 2)
    finish(0, 0, Z.at[1])
    finish(0, 1, jac)
    jac[...] = 1.0 / jac[...]
    V[0] = jac[...] * Z[1]

    def step(j, c):
        L[...] = local(V[j])
        prepare(j + 1, 0, L[...])
        send(j + 1, 1)
        products(j, ITERS)
        receive(j + 1, 1)
        finish(j + 1, 0, A.at[j])
        first = j == 0
        gain = jnp.where(first, 1.0 / HALF, 2.0 / HALF)
        z = gain * (A[j] - CENTRE * Z[j + 1]) - jnp.where(first, 0.0, 1.0) * Z[j]
        Z[j + 2] = z
        V[j + 1] = jac[...] * z
        return c

    lax.fori_loop(0, ITERS - 1, step, 0)

    last = ITERS - 1
    L[...] = local(V[last])
    products(last, ITERS)
    sums = jnp.sum(acc[...], axis=1)
    sums = jnp.sum(sums, axis=1, keepdims=True)
    pick = lax.broadcasted_iota(jnp.int32, (24, 128), 0) == lax.broadcasted_iota(jnp.int32, (24, 128), 1)

    def share(row, buf, me, group, n, ss, rs, values):
        row[...] = values
        buf[me] = values

        for k in far_first(n):
            pltpu.make_async_remote_copy(
                src_ref=row, dst_ref=buf.at[me], send_sem=ss, recv_sem=rs,
                device_id=group(k), device_id_type=MESH,
            ).start()
        peers = buf.at[pl.ds(0, n - 1)]
        return lambda: pltpu.make_async_copy(peers, peers, rs).wait(), lambda: pltpu.make_async_copy(peers, peers, ss).wait()

    values = jnp.sum(jnp.where(pick, sums, 0.0), axis=0, keepdims=True)
    arrive_a, left_a = share(row_a, buf_a, my_a, dev_a, plane, ssem_a, rsem_a, values)
    prepare(ITERS, 0, L[...])
    send(ITERS, 1)
    arrive_a()
    values = jnp.sum(buf_a[...], axis=0)
    arrive_b, left_b = share(row_b, buf_b, my_b, dev_b, ring, ssem_b, rsem_b, values)
    receive(ITERS, 1)
    finish(ITERS, 0, A.at[last])
    arrive_b()
    values = jnp.broadcast_to(jnp.sum(buf_b[...], axis=0), (8, 128))

    def value(k):
        return jnp.sum(jnp.where(lane == k, values, 0.0), axis=1, keepdims=True)

    H = [[value(4 * max(i, j) + min(i, j)) for j in range(ITERS)] for i in range(ITERS)]
    g = [value(16 + i) for i in range(ITERS)]
    for k in range(ITERS):
        inv = 1.0 / H[k][k]
        for i in range(k + 1, ITERS):
            f = H[i][k] * inv
            for j in range(k + 1, ITERS):
                H[i][j] = H[i][j] - f * H[k][j]
            g[i] = g[i] - f * g[k]
    y = [None] * ITERS
    for k in reversed(range(ITERS)):
        s = g[k]
        for j in range(k + 1, ITERS):
            s = s - H[k][j] * y[j]
        y[k] = s / H[k][k]

    wide = [jnp.broadcast_to(c, (8, 128))[None] for c in y]
    total = wide[0] * V[0].reshape(32, 8, 128)
    rest = Z[1].reshape(32, 8, 128) - wide[0] * A[0].reshape(32, 8, 128)
    for j in range(1, ITERS):
        total = total + wide[j] * V[j].reshape(32, 8, 128)
        rest = rest - wide[j] * A[j].reshape(32, 8, 128)
    sol_ref[...] = total.reshape(16, 16, 128)
    res_ref[...] = rest.reshape(16, 16, 128)

    sent(0, 2)

    def settle(s, c):
        sent(s, 1)
        return c

    lax.fori_loop(1, ITERS + 1, settle, 0)
    left_a()
    left_b()


def solution(mesh):
    dims = tuple(mesh.shape[a] for a in AXES)
    xwidth = min(4, dims[1] // 2)
    plane, ring = dims[0] * xwidth, dims[1] // xwidth * dims[2]
    steps = ITERS + 1
    f32 = jnp.float32
    block = (16, 16, 128)
    vmem = pl.BlockSpec(memory_space=pltpu.VMEM)
    dma = pltpu.SemaphoreType.DMA

    def body(*args):
        def run(*refs):
            kernel(dims, xwidth, *refs)

        mats, facs = constants()
        return pl.pallas_call(
            run,
            out_shape=[pltpu.VMEM(block, f32)] * 2,
            in_specs=[pl.BlockSpec(memory_space=pltpu.HBM)] * 7,
            out_specs=[vmem] * 2,
            scratch_shapes=[
                *[pltpu.VMEM(block, f32)] * 5,
                pltpu.VMEM(mats.shape, f32),
                pltpu.VMEM(facs.shape, f32),
                pltpu.VMEM(block, f32),
                pltpu.VMEM((steps, 2) + block, f32),
                pltpu.VMEM(block, f32),
                pltpu.VMEM((ITERS,) + block, f32),
                pltpu.VMEM((ITERS + 1,) + block, f32),
                pltpu.VMEM((ITERS,) + block, f32),
                pltpu.VMEM((steps, 2, 2, 16, 128), f32),
                pltpu.VMEM((steps, 2, 8, 128), f32),
                pltpu.VMEM((steps, 2, 2, 16, 128), f32),
                pltpu.VMEM((steps, 2, 2, 16, 128), f32),
                pltpu.VMEM((steps, 2, 2, 8, 128), f32),
                pltpu.VMEM((steps, 2, 4, 8, 128), f32),
                pltpu.VMEM((steps, 2, 16, 128), f32),
                pltpu.VMEM((24, 8, 128), f32),
                pltpu.VMEM((256, 128), f32),
                pltpu.VMEM((1, 128), f32),
                pltpu.VMEM((1, 128), f32),
                pltpu.VMEM((plane, 1, 128), f32),
                pltpu.VMEM((ring, 1, 128), f32),
                dma((steps,)),
                dma((steps,)),
                dma,
                dma,
                dma,
                dma,
                dma((7,)),
            ],
            compiler_params=pltpu.CompilerParams(
                collective_id=0, has_side_effects=True, vmem_limit_bytes=32 * 1024 * 1024
            ),
        )(*(pltpu.with_memory_space_constraint(a, pltpu.HBM) for a in (*args, jnp.asarray(mats), jnp.asarray(facs))))

    spec = P(*AXES)
    return jax.shard_map(
        body, mesh=mesh, in_specs=(spec,) * 5, out_specs=(spec,) * 2, check_vma=False
    )
```

```python
import itertools

import jax
import jax.numpy as jnp
import numpy as np
from jax import lax
from jax.experimental import pallas as pl
from jax.experimental.pallas import tpu as pltpu
from jax.sharding import PartitionSpec as P

MESH = pl.DeviceIdType.MESH
ITERS = 4
CENTRE, HALF = 1.2, 1.1
AXES = ("gx", "gy", "gz")

NEAR = sorted(
    (o for o in itertools.product((-1, 0, 1), repeat=3) if o != (0, 0, 0)),
    key=lambda o: (o[1] == 0, -abs(o[0]) - abs(o[2])),
)


def derivative_table():
    points = np.array(
        [
            -1.0,
            -0.8717401485096066,
            -0.5917001814331423,
            -0.2092992179024789,
            0.2092992179024789,
            0.5917001814331423,
            0.8717401485096066,
            1.0,
        ]
    )
    gaps = points[:, None] - points[None, :] + np.eye(8)
    weights_c = np.prod(gaps, axis=1)
    table = weights_c[:, None] / (weights_c[None, :] * gaps)
    table = table - np.diag(np.diag(table))
    return table - np.diag(table.sum(axis=1))


TABLE = derivative_table()


def sublane_factors(matrix):
    k = np.arange(8)
    rows = np.stack([matrix[k, (k + s) % 8] for s in range(8)])
    return np.repeat(rows[:, :, None], 128, axis=2)


def constants():
    square = (TABLE * TABLE).T
    mats = [np.kron(np.eye(16), m.T) for m in (TABLE, TABLE.T, square)]
    facs = [sublane_factors(m) for m in (TABLE, TABLE.T, square)]
    return np.stack(mats).astype(np.float32), np.stack(facs).astype(np.float32)


def along_x(field, matrix):
    out = [None] * 16
    for base in (0, 8):
        even = [field[base + i] + field[base + 7 - i] for i in range(4)]
        odd = [field[base + i] - field[base + 7 - i] for i in range(4)]
        for k in range(4):
            e = sum(float(0.5 * (matrix[k, i] + matrix[k, 7 - i])) * even[i] for i in range(4))
            o = sum(float(0.5 * (matrix[k, i] - matrix[k, 7 - i])) * odd[i] for i in range(4))
            out[base + k] = o + e
            out[base + 7 - k] = o - e
    return out


def along_x_plain(field, matrix):
    return [
        sum(float(matrix[k % 8, i]) * field[k // 8 * 8 + i] for i in range(8)) for k in range(16)
    ]


def along_y(field, facs):
    total = field * facs[0][None]
    for s in range(1, 8):
        total = total + pltpu.roll(field, 8 - s, 1) * facs[s][None]
    return total


def along_z(field, mat):
    flat = field.reshape(-1, 128)
    return jnp.dot(flat, mat, precision=lax.Precision.HIGHEST, preferred_element_type=jnp.float32)


def slabs(field):
    return [field[i] for i in range(16)]


def kernel(
    dims, xwidth,
    src_hbm, mx_hbm, my_hbm, mz_hbm, mass_hbm, mats_hbm, facs_hbm,
    sol_ref, res_ref,
    src_ref, mx_ref, my_ref, mz_ref, mass_ref, mats_ref, facs_ref,
    jac, T, L, V, Z, A, YS, PS, PR, FC, XF, YF, ZF, XZ, RB, acc, count, row_a, row_b, buf_a, buf_b,
    ssem, rsem, ssem_a, rsem_a, ssem_b, rsem_b, lsem,
):
    nx, ny, nz = dims
    ix, iy, iz = (lax.axis_index(a) for a in AXES)
    here = {0: (ix, nx), 1: (iy, ny), 2: (iz, nz)}

    def exists(o):
        ok = None
        for d in range(3):
            at, n = here[d]
            c = at > 0 if o[d] < 0 else at < n - 1 if o[d] > 0 else None
            ok = c if ok is None else ok if c is None else jnp.logical_and(ok, c)
        return ok

    def dev(o):
        return (ix + o[0], iy + o[1], iz + o[2])

    depth = ny // xwidth
    plane, ring = nx * xwidth, depth * nz
    col, high = lax.rem(iy, xwidth), iy // xwidth
    my_a = ix * xwidth + col
    my_b = high * nz + iz

    def carry(at, by, n):
        to = at + by
        over = to >= n
        return jnp.where(over, to - n, to), over.astype(jnp.int32)

    def dev_a(k):
        x, up = carry(col, k % xwidth, xwidth)
        return carry(ix, k // xwidth + up, nx)[0], high * xwidth + x, iz

    def dev_b(k):
        z, up = carry(iz, k % nz, nz)
        return ix, carry(high, k // nz + up, depth)[0] * xwidth + col, z

    def far_first(n):
        return sorted(range(1, n), key=lambda k: abs(2 * k - n))

    loads = [
        pltpu.make_async_copy(a, b, lsem.at[i])
        for i, (a, b) in enumerate(
            (
                (src_hbm, src_ref),
                (mats_hbm, mats_ref),
                (facs_hbm, facs_ref),
                (mx_hbm, mx_ref),
                (my_hbm, my_ref),
                (mz_hbm, mz_ref),
                (mass_hbm, mass_ref),
            )
        )
    ]
    for load in loads:
        load.start()
    for ref in (XF, YF, ZF, XZ, RB):
        ref[0] = jnp.zeros(ref.shape[1:], jnp.float32)
    barrier = pltpu.get_barrier_semaphore()

    def greet(group, n):
        for k in far_first(n):
            pl.semaphore_signal(barrier, inc=1, device_id=group(k), device_id_type=MESH)

    greet(dev_b, ring)
    for o in NEAR:
        @pl.when(exists(o))
        def _(o=o):
            pl.semaphore_signal(barrier, inc=1, device_id=dev(o), device_id_type=MESH)
    greet(dev_a, plane)
    sides = [1 + (at > 0).astype(jnp.int32) + (at < n - 1).astype(jnp.int32) for at, n in here.values()]
    n_near = sides[0] * sides[1] * sides[2] - 1

    lane = lax.broadcasted_iota(jnp.int32, (8, 128), 1)
    within = lax.rem(lane, 8)
    close = jnp.where((within == 7) & (lane != 127), 1.0, 0.0)[None]
    opens = jnp.where((within == 0) & (lane != 0), 1.0, 0.0)[None]
    even = lax.rem(lane, 2) == 0
    ends_z = (lane == 0) | (lane == 127)

    lane16 = lax.broadcasted_iota(jnp.int32, (16, 128), 1)
    row16 = lax.broadcasted_iota(jnp.int32, (16, 128), 0)

    def rows(ref):
        return ref[:, 0, :], ref[:, 15, :]

    def add_rows(ref, parts):
        ref[:, 0, :] = ref[:, 0, :] + parts[0]
        ref[:, 15, :] = ref[:, 15, :] + parts[1]

    def inside(v):
        return v + pltpu.roll(v, 127, 2) * close + pltpu.roll(v, 1, 2) * opens

    def prepare(s, f, raw, faces):
        v = raw.reshape(32, 8, 128)
        v = inside(v)
        t = T.at[s, f]
        t[...] = v.reshape(16, 16, 128)
        both = t[7] + t[8]
        t[7] = both
        t[8] = both
        both = t[:, 7, :] + t[:, 8, :]
        t[:, 7, :] = both
        t[:, 8, :] = both
        if faces:
            YS[s, f, 0], YS[s, f, 1] = rows(t)
        packed = jnp.zeros((8, 128), jnp.float32)
        for i in range(32):
            tile = t[i // 2, pl.ds(8 * (i % 2), 8), :]
            packed = jnp.where(lane // 2 == i, pltpu.roll(tile, 2 * i + 1, 1), packed)
        PS[s, f] = packed
        if faces:
            PR[s, f, pl.ds(0, 1)] = packed[0:1]
            PR[s, f, pl.ds(1, 1)] = packed[7:8]

    def prepare_faces(s, parts):
        v = inside(jnp.concatenate(parts, axis=0).reshape(4, 8, 128))
        ys = YS.at[s, 0]
        ys[...] = v.reshape(2, 16, 128)
        for e in (0, 1):
            both = ys[e, pl.ds(7, 1), :] + ys[e, pl.ds(8, 1), :]
            ys[e, pl.ds(7, 1), :] = both
            ys[e, pl.ds(8, 1), :] = both
            face = ys[e]
            to = 4 * row16 + 2 * e
            line = jnp.where(lane16 == to, face[:, 127:128], 0.0)
            line = jnp.where(lane16 == to + 1, face[:, 0:1], line)
            PR[s, 0, pl.ds(e, 1)] = jnp.sum(line, axis=0, keepdims=True)

    def end(d):
        return 0 if d < 0 else 1

    def copies(s, fields, far):
        fs = pl.ds(0, fields)
        for o in NEAR:
            dx, dy, dz = o
            if (dy != 0) != far:
                continue
            ex, ey, ez = end(-dx), end(-dy), end(-dz)
            if dz == 0:
                if dy == 0:
                    src, dst = T.at[s, fs, 15 * end(dx)], XF.at[s, fs, ex]
                elif dx == 0:
                    src, dst = YS.at[s, fs, end(dy)], YF.at[s, fs, ey]
                else:
                    src = YS.at[s, fs, end(dy), pl.ds(15 * end(dx), 1)]
                    dst = RB.at[s, fs, pl.ds(2 * ex + ey, 1)]
            elif dy == 0:
                src = PS.at[s, fs]
                dst = ZF.at[s, fs, ez] if dx == 0 else XZ.at[s, fs, 2 * ex + ez]
            else:
                src = PR.at[s, fs, pl.ds(end(dy), 1)]
                slot = 4 + 2 * ey + ez if dx == 0 else 8 + 4 * ex + 2 * ey + ez
                dst = RB.at[s, fs, pl.ds(slot, 1)]
            yield o, pltpu.make_async_remote_copy(
                src_ref=src, dst_ref=dst, send_sem=ssem.at[s, int(far)], recv_sem=rsem.at[s, int(far)],
                device_id=dev(o), device_id_type=MESH,
            )

    def send(s, fields, far):
        for o, copy in copies(s, fields, far):
            pl.when(exists(o))(copy.start)

    def wait_all(sem, fields, far):
        for cx, cy, cz in itertools.product((1, 2), (1, 2) if far else (0,), (1, 2)):
            if far:
                total = 16 * cy + cx * cy + cy * cz * (1 + cx)
            else:
                total = 16 * cx + 8 * cz + 8 * cx * cz
            match = (sides[0] == cx + 1) & (sides[2] == cz + 1)
            if far:
                match = match & (sides[1] == cy + 1)

            @pl.when(match)
            def _(total=total):
                whole = count.at[pl.ds(0, total * fields)]
                pltpu.make_async_copy(whole, whole, sem).wait()

    def receive(s, fields, far):
        wait_all(rsem.at[s, int(far)], fields, far)

    def sent(s, fields):
        for far in (True, False):
            wait_all(ssem.at[s, int(far)], fields, far)

    def merge(minus, plus):
        return jnp.where(even, pltpu.roll(plus, 127, 1), pltpu.roll(minus, 1, 1))

    def shifted(m, minus, plus):
        m = m + jnp.where(lane < 4, pltpu.roll(minus, 68, 1), 0.0)
        return m + jnp.where((lane >= 60) & (lane < 64), pltpu.roll(plus, 60, 1), 0.0)

    def finish_near(s, f, out):
        m = merge(ZF[s, f, 0], ZF[s, f, 1])
        m = shifted(m, merge(XZ[s, f, 0], XZ[s, f, 1]), merge(XZ[s, f, 2], XZ[s, f, 3]))
        for i in range(32):
            at = (i // 2, pl.ds(8 * (i % 2), 8), slice(None))
            part = jnp.where(ends_z, pltpu.roll(m, 127 - 2 * i, 1), 0.0)
            out[at] = T[(s, f) + at] + part
        for e in (0, 1):
            out[15 * e] = out[15 * e] + XF[s, f, e]

    def from_far(s, f):
        rb = RB.at[s, f]

        def line(k):
            return jnp.broadcast_to(rb[pl.ds(k, 1), :], (8, 128))

        parts = []
        for e in (0, 1):
            m, minus, plus = (merge(line(k + 2 * e), line(k + 2 * e + 1)) for k in (4, 8, 12))
            m = jnp.broadcast_to(shifted(m, minus, plus)[0:1], (16, 128))
            at = 4 * row16 + 2 * (1 - e)
            last = jnp.sum(jnp.where(lane16 == at, m, 0.0), axis=1, keepdims=True)
            first = jnp.sum(jnp.where(lane16 == at + 1, m, 0.0), axis=1, keepdims=True)
            part = YF[s, f, e]
            part = part + jnp.where(row16 == 0, rb[pl.ds(e, 1), :], 0.0)
            part = part + jnp.where(row16 == 15, rb[pl.ds(2 + e, 1), :], 0.0)
            part = part + jnp.where(lane16 == 0, first, 0.0) + jnp.where(lane16 == 127, last, 0.0)
            parts.append(part)
        return parts

    def finish(s, f, out):
        finish_near(s, f, out)
        add_rows(out, from_far(s, f))

    def local_y(v):
        v3 = v.reshape(32, 8, 128)
        slope = my_ref[...].reshape(32, 8, 128) * along_y(v3, facs_ref[0])
        return mass_ref[...] * v + along_y(slope, facs_ref[1]).reshape(16, 16, 128)

    def local_faces(parts, gains):
        flat = jnp.concatenate(parts, axis=0)
        slope = gains[0].reshape(4, 8, 128) * along_y(flat.reshape(4, 8, 128), facs_ref[0])
        total = along_y(slope, facs_ref[1]).reshape(32, 128)
        total = total + along_z(gains[1] * along_z(flat, mats_ref[0]), mats_ref[1])
        return total[:16], total[16:]

    def local(v):
        total = local_y(v)
        slope = along_x(slabs(v), TABLE)
        slope = [mx_ref[i] * slope[i] for i in range(16)]
        total = total + jnp.stack(along_x(slope, TABLE.T))
        slope = mz_ref[...].reshape(256, 128) * along_z(v, mats_ref[0])
        return total + along_z(slope, mats_ref[1]).reshape(16, 16, 128)

    def product(slot, a, b):
        acc[slot] = jnp.sum((a * b).reshape(32, 8, 128), axis=0)

    def products(j, upto):
        for i in range(upto):
            product(4 * j + i, L[...], V[i])
        product(16 + j, src_ref[...], V[j])

    for ref in (XF, YF, ZF, XZ, RB):
        ref[1:] = jnp.zeros((ITERS,) + ref.shape[1:], jnp.float32)
    V[...] = jnp.zeros_like(V)
    acc[...] = jnp.zeros_like(acc)
    Z[0] = jnp.zeros((16, 16, 128), jnp.float32)
    loads[0].wait()
    prepare(0, 0, src_ref[...], True)
    for load in loads[1:]:
        load.wait()
    diag = mass_ref[...] + jnp.stack(along_x_plain(slabs(mx_ref[...]), (TABLE * TABLE).T))
    L[...] = along_y(my_ref[...].reshape(32, 8, 128), facs_ref[2]).reshape(16, 16, 128)
    diag = diag + L[...]
    diag = diag + along_z(mz_ref[...], mats_ref[2]).reshape(16, 16, 128)
    prepare(0, 1, diag, True)
    pl.semaphore_wait(barrier, n_near + (plane - 1) + (ring - 1))
    send(0, 2, True)
    send(0, 2, False)
    both = [jnp.concatenate(rows(ref), axis=0) for ref in (mx_ref, mz_ref)]
    FC[0], FC[1] = both
    FC[2] = jnp.concatenate([a + b for a, b in zip(rows(mass_ref), rows(L))], axis=0)
    receive(0, 2, False)
    receive(0, 2, True)
    finish(0, 0, Z.at[1])
    finish(0, 1, jac)
    jac[...] = 1.0 / jac[...]
    V[0] = jac[...] * Z[1]
    L[...] = local_y(V[0])
    more = local_faces(rows(V.at[0]), (FC[0], FC[1]))
    prepare_faces(1, [a + b for a, b in zip(rows(L), more)])
    send(1, 1, True)

    for j in range(ITERS - 1):
        s = j + 1
        L[...] = local(V[j])
        prepare(s, 0, L[...], False)
        send(s, 1, False)
        products(j, ITERS)
        receive(s, 1, False)
        finish_near(s, 0, A.at[j])
        gain = (1.0 if j == 0 else 2.0) / HALF
        z = gain * (A[j] - CENTRE * Z[j + 1]) - (0.0 if j == 0 else 1.0) * Z[j]
        Z[j + 2] = z
        V[j + 1] = jac[...] * z
        if j < ITERS - 2:
            L[...] = local_y(V[j + 1])
        receive(s, 1, True)
        d_image = from_far(s, 0)
        d_base = [gain * d for d in d_image]
        d_smooth = [a * b for a, b in zip(rows(jac), d_base)]
        if j < ITERS - 2:
            more = local_faces([a + b for a, b in zip(rows(V.at[j + 1]), d_smooth)], (FC[0], FC[1]))
            own = [FC[2, pl.ds(16 * e, 16)] * d_smooth[e] for e in (0, 1)]
            prepare_faces(s + 1, [a + b + c for a, b, c in zip(rows(L), more, own)])
            send(s + 1, 1, True)
        add_rows(A.at[j], d_image)
        add_rows(Z.at[j + 2], d_base)
        add_rows(V.at[j + 1], d_smooth)

    last = ITERS - 1
    L[...] = local(V[last])
    products(last, ITERS)
    sums = jnp.sum(acc[...], axis=1)
    sums = jnp.sum(sums, axis=1, keepdims=True)
    pick = lax.broadcasted_iota(jnp.int32, (24, 128), 0) == lax.broadcasted_iota(jnp.int32, (24, 128), 1)

    def share(row, buf, me, group, n, ss, rs, values):
        row[...] = values
        buf[me] = values

        for k in far_first(n):
            pltpu.make_async_remote_copy(
                src_ref=row, dst_ref=buf.at[me], send_sem=ss, recv_sem=rs,
                device_id=group(k), device_id_type=MESH,
            ).start()
        peers = buf.at[pl.ds(0, n - 1)]
        return lambda: pltpu.make_async_copy(peers, peers, rs).wait(), lambda: pltpu.make_async_copy(peers, peers, ss).wait()

    values = jnp.sum(jnp.where(pick, sums, 0.0), axis=0, keepdims=True)
    arrive_a, left_a = share(row_a, buf_a, my_a, dev_a, plane, ssem_a, rsem_a, values)
    prepare(ITERS, 0, L[...], True)
    send(ITERS, 1, True)
    send(ITERS, 1, False)
    arrive_a()
    values = jnp.sum(buf_a[...], axis=0)
    arrive_b, left_b = share(row_b, buf_b, my_b, dev_b, ring, ssem_b, rsem_b, values)
    receive(ITERS, 1, False)
    receive(ITERS, 1, True)
    finish(ITERS, 0, A.at[last])
    sent(0, 2)

    def settle(s, c):
        sent(s, 1)
        return c

    lax.fori_loop(1, ITERS + 1, settle, 0)
    left_a()
    arrive_b()
    values = jnp.broadcast_to(jnp.sum(buf_b[...], axis=0), (8, 128))

    def value(k):
        return jnp.sum(jnp.where(lane == k, values, 0.0), axis=1, keepdims=True)

    H = [[value(4 * max(i, j) + min(i, j)) for j in range(ITERS)] for i in range(ITERS)]
    g = [value(16 + i) for i in range(ITERS)]
    for k in range(ITERS):
        inv = 1.0 / H[k][k]
        for i in range(k + 1, ITERS):
            f = H[i][k] * inv
            for j in range(k + 1, ITERS):
                H[i][j] = H[i][j] - f * H[k][j]
            g[i] = g[i] - f * g[k]
    y = [None] * ITERS
    for k in reversed(range(ITERS)):
        s = g[k]
        for j in range(k + 1, ITERS):
            s = s - H[k][j] * y[j]
        y[k] = s / H[k][k]

    wide = [jnp.broadcast_to(c, (8, 128))[None] for c in y]
    total = wide[0] * V[0].reshape(32, 8, 128)
    rest = Z[1].reshape(32, 8, 128) - wide[0] * A[0].reshape(32, 8, 128)
    for j in range(1, ITERS):
        total = total + wide[j] * V[j].reshape(32, 8, 128)
        rest = rest - wide[j] * A[j].reshape(32, 8, 128)
    sol_ref[...] = total.reshape(16, 16, 128)
    res_ref[...] = rest.reshape(16, 16, 128)

    left_b()


def solution(mesh):
    dims = tuple(mesh.shape[a] for a in AXES)
    xwidth = min(4, dims[1] // 2)
    plane, ring = dims[0] * xwidth, dims[1] // xwidth * dims[2]
    steps = ITERS + 1
    f32 = jnp.float32
    block = (16, 16, 128)
    vmem = pl.BlockSpec(memory_space=pltpu.VMEM)
    dma = pltpu.SemaphoreType.DMA

    def body(*args):
        def run(*refs):
            kernel(dims, xwidth, *refs)

        mats, facs = constants()
        return pl.pallas_call(
            run,
            out_shape=[pltpu.VMEM(block, f32)] * 2,
            in_specs=[pl.BlockSpec(memory_space=pltpu.HBM)] * 7,
            out_specs=[vmem] * 2,
            scratch_shapes=[
                *[pltpu.VMEM(block, f32)] * 5,
                pltpu.VMEM(mats.shape, f32),
                pltpu.VMEM(facs.shape, f32),
                pltpu.VMEM(block, f32),
                pltpu.VMEM((steps, 2) + block, f32),
                pltpu.VMEM(block, f32),
                pltpu.VMEM((ITERS,) + block, f32),
                pltpu.VMEM((ITERS + 1,) + block, f32),
                pltpu.VMEM((ITERS,) + block, f32),
                pltpu.VMEM((steps, 2, 2, 16, 128), f32),
                pltpu.VMEM((steps, 2, 8, 128), f32),
                pltpu.VMEM((steps, 2, 8, 128), f32),
                pltpu.VMEM((3, 32, 128), f32),
                pltpu.VMEM((steps, 2, 2, 16, 128), f32),
                pltpu.VMEM((steps, 2, 2, 16, 128), f32),
                pltpu.VMEM((steps, 2, 2, 8, 128), f32),
                pltpu.VMEM((steps, 2, 4, 8, 128), f32),
                pltpu.VMEM((steps, 2, 16, 128), f32),
                pltpu.VMEM((24, 8, 128), f32),
                pltpu.VMEM((256, 128), f32),
                pltpu.VMEM((1, 128), f32),
                pltpu.VMEM((1, 128), f32),
                pltpu.VMEM((plane, 1, 128), f32),
                pltpu.VMEM((ring, 1, 128), f32),
                dma((steps, 2)),
                dma((steps, 2)),
                dma,
                dma,
                dma,
                dma,
                dma((7,)),
            ],
            compiler_params=pltpu.CompilerParams(
                collective_id=0, has_side_effects=True, vmem_limit_bytes=32 * 1024 * 1024
            ),
        )(*(pltpu.with_memory_space_constraint(a, pltpu.HBM) for a in (*args, jnp.asarray(mats), jnp.asarray(facs))))

    spec = P(*AXES)
    return jax.shard_map(
        body, mesh=mesh, in_specs=(spec,) * 5, out_specs=(spec,) * 2, check_vma=False
    )
```

```python
import itertools

import jax
import jax.numpy as jnp
import numpy as np
from jax import lax
from jax.experimental import pallas as pl
from jax.experimental.pallas import tpu as pltpu
from jax.sharding import PartitionSpec as P

MESH = pl.DeviceIdType.MESH
ITERS = 4
CENTRE, HALF = 1.2, 1.1
AXES = ("gx", "gy", "gz")

NEAR = sorted(
    (o for o in itertools.product((-1, 0, 1), repeat=3) if o != (0, 0, 0)),
    key=lambda o: (o[1] == 0, -abs(o[0]) - abs(o[2])),
)


def derivative_table():
    points = np.array(
        [
            -1.0,
            -0.8717401485096066,
            -0.5917001814331423,
            -0.2092992179024789,
            0.2092992179024789,
            0.5917001814331423,
            0.8717401485096066,
            1.0,
        ]
    )
    gaps = points[:, None] - points[None, :] + np.eye(8)
    weights_c = np.prod(gaps, axis=1)
    table = weights_c[:, None] / (weights_c[None, :] * gaps)
    table = table - np.diag(np.diag(table))
    return table - np.diag(table.sum(axis=1))


TABLE = derivative_table()


def sublane_factors(matrix):
    k = np.arange(8)
    rows = np.stack([matrix[k, (k + s) % 8] for s in range(8)])
    return np.repeat(rows[:, :, None], 128, axis=2)


def lane_factors(matrix):
    k = np.arange(128)
    rows = np.zeros((16, 128))
    for s in range(-7, 8):
        to = k % 8 + s
        rows[7 + s] = np.where((to >= 0) & (to < 8), matrix[k % 8, np.clip(to, 0, 7)], 0.0)
    return rows


def constants():
    square = (TABLE * TABLE).T
    mats = [np.kron(np.eye(16), m.T) for m in (TABLE, TABLE.T, square)]
    facs = [sublane_factors(m) for m in (TABLE, TABLE.T, square)]
    lanes = [lane_factors(m) for m in (TABLE, TABLE.T)]
    return tuple(np.stack(a).astype(np.float32) for a in (mats, facs, lanes))


def along_x(field, matrix):
    out = [None] * 16
    for base in (0, 8):
        even = [field[base + i] + field[base + 7 - i] for i in range(4)]
        odd = [field[base + i] - field[base + 7 - i] for i in range(4)]
        for k in range(4):
            e = sum(float(0.5 * (matrix[k, i] + matrix[k, 7 - i])) * even[i] for i in range(4))
            o = sum(float(0.5 * (matrix[k, i] - matrix[k, 7 - i])) * odd[i] for i in range(4))
            out[base + k] = o + e
            out[base + 7 - k] = o - e
    return out


def along_x_plain(field, matrix):
    return [
        sum(float(matrix[k % 8, i]) * field[k // 8 * 8 + i] for i in range(8)) for k in range(16)
    ]


def along_y(field, facs):
    total = field * facs[0][None]
    for s in range(1, 8):
        total = total + pltpu.roll(field, 8 - s, 1) * facs[s][None]
    return total


def along_lanes(field, facs):
    parts = [field * facs[pl.ds(7, 1), :][None]]
    for s in range(-7, 8):
        if s != 0:
            parts.append(pltpu.roll(field, -s % 128, 2) * facs[pl.ds(7 + s, 1), :][None])
    while len(parts) > 1:
        parts = [sum(parts[i : i + 2]) for i in range(0, len(parts), 2)]
    return parts[0]


def along_z(field, mat):
    flat = field.reshape(-1, 128)
    return jnp.dot(flat, mat, precision=lax.Precision.HIGHEST, preferred_element_type=jnp.float32)


def slabs(field):
    return [field[i] for i in range(16)]


def kernel(
    dims, xwidth,
    src_hbm, mx_hbm, my_hbm, mz_hbm, mass_hbm, mats_hbm, facs_hbm, lanes_hbm,
    sol_ref, res_ref,
    src_ref, mx_ref, my_ref, mz_ref, mass_ref, mats_ref, facs_ref, lanes_ref,
    jac, T, Y, L, V, Z, A, YS, PS, PR, FC, XF, YF, ZF, XZ, RB, acc, count, row_a, row_b, buf_a, buf_b,
    ssem, rsem, ssem_a, rsem_a, ssem_b, rsem_b, lsem,
):
    nx, ny, nz = dims
    ix, iy, iz = (lax.axis_index(a) for a in AXES)
    here = {0: (ix, nx), 1: (iy, ny), 2: (iz, nz)}

    def exists(o):
        ok = None
        for d in range(3):
            at, n = here[d]
            c = at > 0 if o[d] < 0 else at < n - 1 if o[d] > 0 else None
            ok = c if ok is None else ok if c is None else jnp.logical_and(ok, c)
        return ok

    def dev(o):
        return (ix + o[0], iy + o[1], iz + o[2])

    depth = ny // xwidth
    plane, ring = nx * xwidth, depth * nz
    col, high = lax.rem(iy, xwidth), iy // xwidth
    my_a = ix * xwidth + col
    my_b = high * nz + iz

    def carry(at, by, n):
        to = at + by
        over = to >= n
        return jnp.where(over, to - n, to), over.astype(jnp.int32)

    def dev_a(k):
        x, up = carry(col, k % xwidth, xwidth)
        return carry(ix, k // xwidth + up, nx)[0], high * xwidth + x, iz

    def dev_b(k):
        z, up = carry(iz, k % nz, nz)
        return ix, carry(high, k // nz + up, depth)[0] * xwidth + col, z

    def far_first(n):
        return sorted(range(1, n), key=lambda k: abs(2 * k - n))

    loads = [
        pltpu.make_async_copy(a, b, lsem.at[i])
        for i, (a, b) in enumerate(
            (
                (src_hbm, src_ref),
                (mats_hbm, mats_ref),
                (facs_hbm, facs_ref),
                (mx_hbm, mx_ref),
                (my_hbm, my_ref),
                (mz_hbm, mz_ref),
                (mass_hbm, mass_ref),
                (lanes_hbm, lanes_ref),
            )
        )
    ]
    for load in loads:
        load.start()
    for ref in (XF, YF, ZF, XZ, RB):
        ref[0] = jnp.zeros(ref.shape[1:], jnp.float32)
    barrier = pltpu.get_barrier_semaphore()

    def greet(group, n):
        for k in far_first(n):
            pl.semaphore_signal(barrier, inc=1, device_id=group(k), device_id_type=MESH)

    greet(dev_b, ring)
    for o in NEAR:
        @pl.when(exists(o))
        def _(o=o):
            pl.semaphore_signal(barrier, inc=1, device_id=dev(o), device_id_type=MESH)
    greet(dev_a, plane)
    sides = [1 + (at > 0).astype(jnp.int32) + (at < n - 1).astype(jnp.int32) for at, n in here.values()]
    n_near = sides[0] * sides[1] * sides[2] - 1

    lane = lax.broadcasted_iota(jnp.int32, (8, 128), 1)
    within = lax.rem(lane, 8)
    close = jnp.where((within == 7) & (lane != 127), 1.0, 0.0)[None]
    opens = jnp.where((within == 0) & (lane != 0), 1.0, 0.0)[None]
    even = lax.rem(lane, 2) == 0
    ends_z = (lane == 0) | (lane == 127)

    lane16 = lax.broadcasted_iota(jnp.int32, (16, 128), 1)
    row16 = lax.broadcasted_iota(jnp.int32, (16, 128), 0)

    def rows(ref):
        return ref[:, 0, :], ref[:, 15, :]

    def add_rows(ref, parts):
        ref[:, 0, :] = ref[:, 0, :] + parts[0]
        ref[:, 15, :] = ref[:, 15, :] + parts[1]

    def set_rows(ref, parts):
        ref[:, 0, :] = parts[0]
        ref[:, 15, :] = parts[1]

    def inside(v):
        return v + pltpu.roll(v, 127, 2) * close + pltpu.roll(v, 1, 2) * opens

    def prepare(s, f, raw, faces):
        v = raw.reshape(32, 8, 128)
        v = inside(v)
        t = T.at[s, f]
        t[...] = v.reshape(16, 16, 128)
        both = t[7] + t[8]
        t[7] = both
        t[8] = both
        both = t[:, 7, :] + t[:, 8, :]
        t[:, 7, :] = both
        t[:, 8, :] = both
        if faces:
            YS[s, f, 0], YS[s, f, 1] = rows(t)
        packed = jnp.zeros((8, 128), jnp.float32)
        for i in range(32):
            tile = t[i // 2, pl.ds(8 * (i % 2), 8), :]
            packed = jnp.where(lane // 2 == i, pltpu.roll(tile, 2 * i + 1, 1), packed)
        PS[s, f] = packed
        if faces:
            PR[s, f, pl.ds(0, 1)] = packed[0:1]
            PR[s, f, pl.ds(1, 1)] = packed[7:8]

    def prepare_faces(s, parts):
        v = inside(jnp.concatenate(parts, axis=0).reshape(4, 8, 128))
        ys = YS.at[s, 0]
        ys[...] = v.reshape(2, 16, 128)
        for e in (0, 1):
            both = ys[e, pl.ds(7, 1), :] + ys[e, pl.ds(8, 1), :]
            ys[e, pl.ds(7, 1), :] = both
            ys[e, pl.ds(8, 1), :] = both
            face = ys[e]
            to = 4 * row16 + 2 * e
            line = jnp.where(lane16 == to, face[:, 127:128], 0.0)
            line = jnp.where(lane16 == to + 1, face[:, 0:1], line)
            PR[s, 0, pl.ds(e, 1)] = jnp.sum(line, axis=0, keepdims=True)

    def end(d):
        return 0 if d < 0 else 1

    def copies(s, fields, far):
        fs = pl.ds(0, fields)
        for o in NEAR:
            dx, dy, dz = o
            if (dy != 0) != far:
                continue
            ex, ey, ez = end(-dx), end(-dy), end(-dz)
            if dz == 0:
                if dy == 0:
                    src, dst = T.at[s, fs, 15 * end(dx)], XF.at[s, fs, ex]
                elif dx == 0:
                    src, dst = YS.at[s, fs, end(dy)], YF.at[s, fs, ey]
                else:
                    src = YS.at[s, fs, end(dy), pl.ds(15 * end(dx), 1)]
                    dst = RB.at[s, fs, pl.ds(2 * ex + ey, 1)]
            elif dy == 0:
                src = PS.at[s, fs]
                dst = ZF.at[s, fs, ez] if dx == 0 else XZ.at[s, fs, 2 * ex + ez]
            else:
                src = PR.at[s, fs, pl.ds(end(dy), 1)]
                slot = 4 + 2 * ey + ez if dx == 0 else 8 + 4 * ex + 2 * ey + ez
                dst = RB.at[s, fs, pl.ds(slot, 1)]
            yield o, pltpu.make_async_remote_copy(
                src_ref=src, dst_ref=dst, send_sem=ssem.at[s, int(far)], recv_sem=rsem.at[s, int(far)],
                device_id=dev(o), device_id_type=MESH,
            )

    def send(s, fields, far):
        for o, copy in copies(s, fields, far):
            pl.when(exists(o))(copy.start)

    def wait_all(sem, fields, far):
        for cx, cy, cz in itertools.product((1, 2), (1, 2) if far else (0,), (1, 2)):
            if far:
                total = 16 * cy + cx * cy + cy * cz * (1 + cx)
            else:
                total = 16 * cx + 8 * cz + 8 * cx * cz
            match = (sides[0] == cx + 1) & (sides[2] == cz + 1)
            if far:
                match = match & (sides[1] == cy + 1)

            @pl.when(match)
            def _(total=total):
                whole = count.at[pl.ds(0, total * fields)]
                pltpu.make_async_copy(whole, whole, sem).wait()

    def receive(s, fields, far):
        wait_all(rsem.at[s, int(far)], fields, far)

    def sent(s, fields):
        for far in (True, False):
            wait_all(ssem.at[s, int(far)], fields, far)

    def merge(minus, plus):
        return jnp.where(even, pltpu.roll(plus, 127, 1), pltpu.roll(minus, 1, 1))

    def shifted(m, minus, plus):
        m = m + jnp.where(lane < 4, pltpu.roll(minus, 68, 1), 0.0)
        return m + jnp.where((lane >= 60) & (lane < 64), pltpu.roll(plus, 60, 1), 0.0)

    def finish_near(s, f, out):
        m = merge(ZF[s, f, 0], ZF[s, f, 1])
        m = shifted(m, merge(XZ[s, f, 0], XZ[s, f, 1]), merge(XZ[s, f, 2], XZ[s, f, 3]))
        for i in range(32):
            at = (i // 2, pl.ds(8 * (i % 2), 8), slice(None))
            part = jnp.where(ends_z, pltpu.roll(m, 127 - 2 * i, 1), 0.0)
            out[at] = T[(s, f) + at] + part
        for e in (0, 1):
            out[15 * e] = out[15 * e] + XF[s, f, e]

    def from_far(s, f):
        rb = RB.at[s, f]

        def line(k):
            return jnp.broadcast_to(rb[pl.ds(k, 1), :], (8, 128))

        parts = []
        for e in (0, 1):
            m, minus, plus = (merge(line(k + 2 * e), line(k + 2 * e + 1)) for k in (4, 8, 12))
            m = jnp.broadcast_to(shifted(m, minus, plus)[0:1], (16, 128))
            at = 4 * row16 + 2 * (1 - e)
            last = jnp.sum(jnp.where(lane16 == at, m, 0.0), axis=1, keepdims=True)
            first = jnp.sum(jnp.where(lane16 == at + 1, m, 0.0), axis=1, keepdims=True)
            part = YF[s, f, e]
            part = part + jnp.where(row16 == 0, rb[pl.ds(e, 1), :], 0.0)
            part = part + jnp.where(row16 == 15, rb[pl.ds(2 + e, 1), :], 0.0)
            part = part + jnp.where(lane16 == 0, first, 0.0) + jnp.where(lane16 == 127, last, 0.0)
            parts.append(part)
        return parts

    def finish(s, f, out):
        finish_near(s, f, out)
        add_rows(out, from_far(s, f))

    def local_y(v):
        v3 = v.reshape(32, 8, 128)
        slope = my_ref[...].reshape(32, 8, 128) * along_y(v3, facs_ref[0])
        return mass_ref[...] * v + along_y(slope, facs_ref[1]).reshape(16, 16, 128)

    def local_faces(parts, gains):
        both = jnp.concatenate(parts, axis=0).reshape(4, 8, 128)
        slope = gains[1].reshape(4, 8, 128) * along_lanes(both, lanes_ref.at[0])
        total = along_lanes(slope, lanes_ref.at[1])
        slope = gains[0].reshape(4, 8, 128) * along_y(both, facs_ref[0])
        total = (total + along_y(slope, facs_ref[1])).reshape(32, 128)
        return total[:16], total[16:]

    def local(v):
        total = local_y(v)
        slope = along_x(slabs(v), TABLE)
        slope = [mx_ref[i] * slope[i] for i in range(16)]
        total = total + jnp.stack(along_x(slope, TABLE.T))
        slope = mz_ref[...].reshape(256, 128) * along_z(v, mats_ref[0])
        return total + along_z(slope, mats_ref[1]).reshape(16, 16, 128)

    def product(slot, a, b):
        acc[slot] = jnp.sum((a * b).reshape(32, 8, 128), axis=0)

    for ref in (XF, YF, ZF, XZ, RB):
        ref[1:] = jnp.zeros((ITERS,) + ref.shape[1:], jnp.float32)
    acc[...] = jnp.zeros_like(acc)
    Z[0] = jnp.zeros((16, 16, 128), jnp.float32)
    loads[0].wait()
    prepare(0, 0, src_ref[...], True)
    for load in loads[1:]:
        load.wait()
    diag = mass_ref[...] + jnp.stack(along_x_plain(slabs(mx_ref[...]), (TABLE * TABLE).T))
    Y[...] = along_y(my_ref[...].reshape(32, 8, 128), facs_ref[2]).reshape(16, 16, 128)
    diag = diag + Y[...]
    diag = diag + along_z(mz_ref[...], mats_ref[2]).reshape(16, 16, 128)
    prepare(0, 1, diag, True)
    pl.semaphore_wait(barrier, n_near + (plane - 1) + (ring - 1))
    send(0, 2, True)
    send(0, 2, False)
    both = [jnp.concatenate(rows(ref), axis=0) for ref in (mx_ref, mz_ref)]
    FC[0], FC[1] = both
    FC[2] = jnp.concatenate([a + b for a, b in zip(rows(mass_ref), rows(Y))], axis=0)
    def far_faces(s, smooth, change):
        more = local_faces(smooth, (FC[0], FC[1]))
        own = [FC[2, pl.ds(16 * e, 16)] * change[e] for e in (0, 1)]
        prepare_faces(s, [a + b + c for a, b, c in zip(rows(Y), more, own)])
        send(s, 1, True)

    receive(0, 2, False)
    finish_near(0, 0, Z.at[1])
    finish_near(0, 1, jac)
    diag_rows = rows(jac)
    jac[...] = 1.0 / jac[...]
    V[0] = jac[...] * Z[1]
    Y[...] = local_y(V[0])
    receive(0, 2, True)
    d_base = from_far(0, 0)
    jac_rows = [1.0 / (a + b) for a, b in zip(diag_rows, from_far(0, 1))]
    smooth = [a * (b + c) for a, b, c in zip(jac_rows, rows(Z.at[1]), d_base)]
    far_faces(1, smooth, [a - b for a, b in zip(smooth, rows(V.at[0]))])
    add_rows(Z.at[1], d_base)
    set_rows(jac, jac_rows)
    set_rows(V.at[0], smooth)

    last = ITERS - 1
    for j in range(last):
        s = j + 1
        L[j] = local(V[j])
        prepare(s, 0, L[j], False)
        send(s, 1, False)
        for i in range(j + 1):
            product(4 * j + i, L[j], V[i])
        product(16 + j, src_ref[...], V[j])
        receive(s, 1, False)
        finish_near(s, 0, A.at[j])
        gain = (1.0 if j == 0 else 2.0) / HALF
        z = gain * (A[j] - CENTRE * Z[j + 1]) - (0.0 if j == 0 else 1.0) * Z[j]
        Z[j + 2] = z
        V[j + 1] = jac[...] * z
        if j < last - 1:
            Y[...] = local_y(V[j + 1])
        else:
            L[last] = local(V[last])
            for i in range(ITERS):
                product(4 * last + i, L[i], V[last])
            product(16 + last, src_ref[...], V[last])
        receive(s, 1, True)
        d_image = from_far(s, 0)
        d_base = [gain * d for d in d_image]
        d_smooth = [a * b for a, b in zip(rows(jac), d_base)]
        if j < last - 1:
            far_faces(s + 1, [a + b for a, b in zip(rows(V.at[j + 1]), d_smooth)], d_smooth)
        else:
            more = local_faces(d_smooth, (FC[0], FC[1]))
            own = [FC[2, pl.ds(16 * e, 16)] * d_smooth[e] + more[e] for e in (0, 1)]

            def add_product(slot, parts):
                part = sum((a * b).reshape(2, 8, 128)[h] for a, b in zip(parts, d_smooth) for h in (0, 1))
                acc[slot] = acc[slot] + part

            for i in range(last):
                add_product(4 * last + i, rows(L.at[i]))
            add_product(5 * last, [2.0 * a + b for a, b in zip(rows(L.at[last]), own)])
            add_product(16 + last, rows(src_ref))
        add_rows(A.at[j], d_image)
        add_rows(Z.at[j + 2], d_base)
        add_rows(V.at[j + 1], d_smooth)

    sums = jnp.sum(acc[...], axis=1)
    sums = jnp.sum(sums, axis=1, keepdims=True)
    pick = lax.broadcasted_iota(jnp.int32, (24, 128), 0) == lax.broadcasted_iota(jnp.int32, (24, 128), 1)

    def share(row, buf, me, group, n, ss, rs, values):
        row[...] = values
        buf[me] = values

        for k in far_first(n):
            pltpu.make_async_remote_copy(
                src_ref=row, dst_ref=buf.at[me], send_sem=ss, recv_sem=rs,
                device_id=group(k), device_id_type=MESH,
            ).start()
        peers = buf.at[pl.ds(0, n - 1)]
        return lambda: pltpu.make_async_copy(peers, peers, rs).wait(), lambda: pltpu.make_async_copy(peers, peers, ss).wait()

    values = jnp.sum(jnp.where(pick, sums, 0.0), axis=0, keepdims=True)
    arrive_a, left_a = share(row_a, buf_a, my_a, dev_a, plane, ssem_a, rsem_a, values)
    prepare(ITERS, 0, local(V[last]), True)
    send(ITERS, 1, True)
    send(ITERS, 1, False)
    arrive_a()
    values = jnp.sum(buf_a[...], axis=0)
    arrive_b, left_b = share(row_b, buf_b, my_b, dev_b, ring, ssem_b, rsem_b, values)
    receive(ITERS, 1, False)
    receive(ITERS, 1, True)
    finish(ITERS, 0, A.at[last])
    sent(0, 2)

    def settle(s, c):
        sent(s, 1)
        return c

    lax.fori_loop(1, ITERS + 1, settle, 0)
    left_a()
    arrive_b()
    values = jnp.broadcast_to(jnp.sum(buf_b[...], axis=0), (8, 128))

    def value(k):
        return jnp.sum(jnp.where(lane == k, values, 0.0), axis=1, keepdims=True)

    H = [[value(4 * max(i, j) + min(i, j)) for j in range(ITERS)] for i in range(ITERS)]
    g = [value(16 + i) for i in range(ITERS)]
    for k in range(ITERS):
        inv = 1.0 / H[k][k]
        for i in range(k + 1, ITERS):
            f = H[i][k] * inv
            for j in range(k + 1, ITERS):
                H[i][j] = H[i][j] - f * H[k][j]
            g[i] = g[i] - f * g[k]
    y = [None] * ITERS
    for k in reversed(range(ITERS)):
        s = g[k]
        for j in range(k + 1, ITERS):
            s = s - H[k][j] * y[j]
        y[k] = s / H[k][k]

    wide = [jnp.broadcast_to(c, (8, 128))[None] for c in y]
    total = wide[0] * V[0].reshape(32, 8, 128)
    rest = Z[1].reshape(32, 8, 128) - wide[0] * A[0].reshape(32, 8, 128)
    for j in range(1, ITERS):
        total = total + wide[j] * V[j].reshape(32, 8, 128)
        rest = rest - wide[j] * A[j].reshape(32, 8, 128)
    sol_ref[...] = total.reshape(16, 16, 128)
    res_ref[...] = rest.reshape(16, 16, 128)

    left_b()


def solution(mesh):
    dims = tuple(mesh.shape[a] for a in AXES)
    xwidth = min(4, dims[1] // 2)
    plane, ring = dims[0] * xwidth, dims[1] // xwidth * dims[2]
    steps = ITERS + 1
    f32 = jnp.float32
    block = (16, 16, 128)
    vmem = pl.BlockSpec(memory_space=pltpu.VMEM)
    dma = pltpu.SemaphoreType.DMA

    def body(*args):
        def run(*refs):
            kernel(dims, xwidth, *refs)

        mats, facs, lanes = constants()
        return pl.pallas_call(
            run,
            out_shape=[pltpu.VMEM(block, f32)] * 2,
            in_specs=[pl.BlockSpec(memory_space=pltpu.HBM)] * 8,
            out_specs=[vmem] * 2,
            scratch_shapes=[
                *[pltpu.VMEM(block, f32)] * 5,
                pltpu.VMEM(mats.shape, f32),
                pltpu.VMEM(facs.shape, f32),
                pltpu.VMEM(lanes.shape, f32),
                pltpu.VMEM(block, f32),
                pltpu.VMEM((steps, 2) + block, f32),
                pltpu.VMEM(block, f32),
                pltpu.VMEM((ITERS,) + block, f32),
                pltpu.VMEM((ITERS,) + block, f32),
                pltpu.VMEM((ITERS + 1,) + block, f32),
                pltpu.VMEM((ITERS,) + block, f32),
                pltpu.VMEM((steps, 2, 2, 16, 128), f32),
                pltpu.VMEM((steps, 2, 8, 128), f32),
                pltpu.VMEM((steps, 2, 8, 128), f32),
                pltpu.VMEM((3, 32, 128), f32),
                pltpu.VMEM((steps, 2, 2, 16, 128), f32),
                pltpu.VMEM((steps, 2, 2, 16, 128), f32),
                pltpu.VMEM((steps, 2, 2, 8, 128), f32),
                pltpu.VMEM((steps, 2, 4, 8, 128), f32),
                pltpu.VMEM((steps, 2, 16, 128), f32),
                pltpu.VMEM((24, 8, 128), f32),
                pltpu.VMEM((256, 128), f32),
                pltpu.VMEM((1, 128), f32),
                pltpu.VMEM((1, 128), f32),
                pltpu.VMEM((plane, 1, 128), f32),
                pltpu.VMEM((ring, 1, 128), f32),
                dma((steps, 2)),
                dma((steps, 2)),
                dma,
                dma,
                dma,
                dma,
                dma((8,)),
            ],
            compiler_params=pltpu.CompilerParams(
                collective_id=0, has_side_effects=True, vmem_limit_bytes=32 * 1024 * 1024
            ),
        )(*(pltpu.with_memory_space_constraint(a, pltpu.HBM) for a in (*args, jnp.asarray(mats), jnp.asarray(facs), jnp.asarray(lanes))))

    spec = P(*AXES)
    return jax.shard_map(
        body, mesh=mesh, in_specs=(spec,) * 5, out_specs=(spec,) * 2, check_vma=False
    )
```

```python
import itertools

import jax
import jax.numpy as jnp
import numpy as np
from jax import lax
from jax.experimental import pallas as pl
from jax.experimental.pallas import tpu as pltpu
from jax.sharding import PartitionSpec as P

MESH = pl.DeviceIdType.MESH
ITERS = 4
CENTRE, HALF = 1.2, 1.1
AXES = ("gx", "gy", "gz")

NEAR = sorted(
    (o for o in itertools.product((-1, 0, 1), repeat=3) if o != (0, 0, 0)),
    key=lambda o: (o[1] == 0, -abs(o[0]) - abs(o[2])),
)


def derivative_table():
    points = np.array(
        [
            -1.0,
            -0.8717401485096066,
            -0.5917001814331423,
            -0.2092992179024789,
            0.2092992179024789,
            0.5917001814331423,
            0.8717401485096066,
            1.0,
        ]
    )
    gaps = points[:, None] - points[None, :] + np.eye(8)
    weights_c = np.prod(gaps, axis=1)
    table = weights_c[:, None] / (weights_c[None, :] * gaps)
    table = table - np.diag(np.diag(table))
    return table - np.diag(table.sum(axis=1))


TABLE = derivative_table()


def sublane_factors(matrix):
    k = np.arange(8)
    rows = np.stack([matrix[k, (k + s) % 8] for s in range(8)])
    return np.repeat(rows[:, :, None], 128, axis=2)


def lane_factors(matrix):
    k = np.arange(128)
    rows = np.zeros((16, 128))
    for s in range(-7, 8):
        to = k % 8 + s
        rows[7 + s] = np.where((to >= 0) & (to < 8), matrix[k % 8, np.clip(to, 0, 7)], 0.0)
    return rows


def constants():
    square = (TABLE * TABLE).T
    mats = [np.kron(np.eye(16), m.T) for m in (TABLE, TABLE.T, square)]
    facs = [sublane_factors(m) for m in (TABLE, TABLE.T, square)]
    lanes = [lane_factors(m) for m in (TABLE, TABLE.T)]
    return tuple(np.stack(a).astype(np.float32) for a in (mats, facs, lanes))


def along_x(field, matrix):
    out = [None] * 16
    for base in (0, 8):
        even = [field[base + i] + field[base + 7 - i] for i in range(4)]
        odd = [field[base + i] - field[base + 7 - i] for i in range(4)]
        for k in range(4):
            e = sum(float(0.5 * (matrix[k, i] + matrix[k, 7 - i])) * even[i] for i in range(4))
            o = sum(float(0.5 * (matrix[k, i] - matrix[k, 7 - i])) * odd[i] for i in range(4))
            out[base + k] = o + e
            out[base + 7 - k] = o - e
    return out


def along_x_plain(field, matrix):
    return [
        sum(float(matrix[k % 8, i]) * field[k // 8 * 8 + i] for i in range(8)) for k in range(16)
    ]


def along_y(field, facs):
    total = field * facs[0][None]
    for s in range(1, 8):
        total = total + pltpu.roll(field, 8 - s, 1) * facs[s][None]
    return total


def along_lanes(field, facs):
    parts = [field * facs[pl.ds(7, 1), :][None]]
    for s in range(-7, 8):
        if s != 0:
            parts.append(pltpu.roll(field, -s % 128, 2) * facs[pl.ds(7 + s, 1), :][None])
    while len(parts) > 1:
        parts = [sum(parts[i : i + 2]) for i in range(0, len(parts), 2)]
    return parts[0]


def along_z(field, mat):
    flat = field.reshape(-1, 128)
    return jnp.dot(flat, mat, precision=lax.Precision.HIGHEST, preferred_element_type=jnp.float32)


def slabs(field):
    return [field[i] for i in range(16)]


def kernel(
    dims, xwidth,
    src_hbm, mx_hbm, my_hbm, mz_hbm, mass_hbm, mats_hbm, facs_hbm, lanes_hbm,
    out_ref,
    src_ref, mx_ref, my_ref, mz_ref, mass_ref, mats_ref, facs_ref, lanes_ref,
    jac, T, Y, L, V, Z, A, YS, PS, PR, FC, XF, YF, ZF, XZ, RB, acc, count, row_a, row_b, buf_a, buf_b,
    ssem, rsem, ssem_a, rsem_a, ssem_b, rsem_b, lsem,
):
    nx, ny, nz = dims
    ix, iy, iz = (lax.axis_index(a) for a in AXES)
    here = {0: (ix, nx), 1: (iy, ny), 2: (iz, nz)}

    def exists(o):
        ok = None
        for d in range(3):
            at, n = here[d]
            c = at > 0 if o[d] < 0 else at < n - 1 if o[d] > 0 else None
            ok = c if ok is None else ok if c is None else jnp.logical_and(ok, c)
        return ok

    def dev(o):
        return (ix + o[0], iy + o[1], iz + o[2])

    depth = ny // xwidth
    plane, ring = nx * xwidth, depth * nz
    col, high = lax.rem(iy, xwidth), iy // xwidth
    my_a = ix * xwidth + col
    my_b = high * nz + iz

    def carry(at, by, n):
        to = at + by
        over = to >= n
        return jnp.where(over, to - n, to), over.astype(jnp.int32)

    def dev_a(k):
        x, up = carry(col, k % xwidth, xwidth)
        return carry(ix, k // xwidth + up, nx)[0], high * xwidth + x, iz

    def dev_b(k):
        z, up = carry(iz, k % nz, nz)
        return ix, carry(high, k // nz + up, depth)[0] * xwidth + col, z

    def far_first(n):
        return sorted(range(1, n), key=lambda k: abs(2 * k - n))

    barrier = pltpu.get_barrier_semaphore()

    def greet(group, n):
        for k in far_first(n):
            pl.semaphore_signal(barrier, inc=1, device_id=group(k), device_id_type=MESH)

    greet(dev_b, ring)
    loads = [
        pltpu.make_async_copy(a, b, lsem.at[i])
        for i, (a, b) in enumerate(
            (
                (src_hbm, src_ref),
                (mats_hbm, mats_ref),
                (facs_hbm, facs_ref),
                (mx_hbm, mx_ref),
                (my_hbm, my_ref),
                (mz_hbm, mz_ref),
                (mass_hbm, mass_ref),
                (lanes_hbm, lanes_ref),
            )
        )
    ]
    for ref in (XF, YF, ZF, XZ, RB):
        ref[0] = jnp.zeros(ref.shape[1:], jnp.float32)
    for o in NEAR:
        @pl.when(exists(o))
        def _(o=o):
            pl.semaphore_signal(barrier, inc=1, device_id=dev(o), device_id_type=MESH)
    greet(dev_a, plane)
    for load in loads:
        load.start()
    sides = [1 + (at > 0).astype(jnp.int32) + (at < n - 1).astype(jnp.int32) for at, n in here.values()]
    n_near = sides[0] * sides[1] * sides[2] - 1

    lane = lax.broadcasted_iota(jnp.int32, (8, 128), 1)
    within = lax.rem(lane, 8)
    close = jnp.where((within == 7) & (lane != 127), 1.0, 0.0)[None]
    opens = jnp.where((within == 0) & (lane != 0), 1.0, 0.0)[None]
    even = lax.rem(lane, 2) == 0
    ends_z = (lane == 0) | (lane == 127)

    lane16 = lax.broadcasted_iota(jnp.int32, (16, 128), 1)
    row16 = lax.broadcasted_iota(jnp.int32, (16, 128), 0)

    def rows(ref):
        return ref[:, 0, :], ref[:, 15, :]

    def add_rows(ref, parts):
        ref[:, 0, :] = ref[:, 0, :] + parts[0]
        ref[:, 15, :] = ref[:, 15, :] + parts[1]

    def set_rows(ref, parts):
        ref[:, 0, :] = parts[0]
        ref[:, 15, :] = parts[1]

    def inside(v):
        return v + pltpu.roll(v, 127, 2) * close + pltpu.roll(v, 1, 2) * opens

    def prepare(s, f, raw, faces):
        v = raw.reshape(32, 8, 128)
        v = inside(v)
        t = T.at[s, f]
        t[...] = v.reshape(16, 16, 128)
        both = t[7] + t[8]
        t[7] = both
        t[8] = both
        both = t[:, 7, :] + t[:, 8, :]
        t[:, 7, :] = both
        t[:, 8, :] = both
        if faces:
            YS[s, f, 0], YS[s, f, 1] = rows(t)
        packed = jnp.zeros((8, 128), jnp.float32)
        for i in range(32):
            tile = t[i // 2, pl.ds(8 * (i % 2), 8), :]
            packed = jnp.where(lane // 2 == i, pltpu.roll(tile, 2 * i + 1, 1), packed)
        PS[s, f] = packed
        if faces:
            PR[s, f, pl.ds(0, 1)] = packed[0:1]
            PR[s, f, pl.ds(1, 1)] = packed[7:8]

    def prepare_faces(s, parts):
        v = inside(jnp.concatenate(parts, axis=0).reshape(4, 8, 128))
        ys = YS.at[s, 0]
        ys[...] = v.reshape(2, 16, 128)
        for e in (0, 1):
            both = ys[e, pl.ds(7, 1), :] + ys[e, pl.ds(8, 1), :]
            ys[e, pl.ds(7, 1), :] = both
            ys[e, pl.ds(8, 1), :] = both
            face = ys[e]
            to = 4 * row16 + 2 * e
            line = jnp.where(lane16 == to, face[:, 127:128], 0.0)
            line = jnp.where(lane16 == to + 1, face[:, 0:1], line)
            PR[s, 0, pl.ds(e, 1)] = jnp.sum(line, axis=0, keepdims=True)

    def end(d):
        return 0 if d < 0 else 1

    def copies(s, fields, far):
        fs = pl.ds(0, fields)
        for o in NEAR:
            dx, dy, dz = o
            if (dy != 0) != far:
                continue
            ex, ey, ez = end(-dx), end(-dy), end(-dz)
            if dz == 0:
                if dy == 0:
                    src, dst = T.at[s, fs, 15 * end(dx)], XF.at[s, fs, ex]
                elif dx == 0:
                    src, dst = YS.at[s, fs, end(dy)], YF.at[s, fs, ey]
                else:
                    src = YS.at[s, fs, end(dy), pl.ds(15 * end(dx), 1)]
                    dst = RB.at[s, fs, pl.ds(2 * ex + ey, 1)]
            elif dy == 0:
                src = PS.at[s, fs]
                dst = ZF.at[s, fs, ez] if dx == 0 else XZ.at[s, fs, 2 * ex + ez]
            else:
                src = PR.at[s, fs, pl.ds(end(dy), 1)]
                slot = 4 + 2 * ey + ez if dx == 0 else 8 + 4 * ex + 2 * ey + ez
                dst = RB.at[s, fs, pl.ds(slot, 1)]
            yield o, pltpu.make_async_remote_copy(
                src_ref=src, dst_ref=dst, send_sem=ssem.at[s, int(far)], recv_sem=rsem.at[s, int(far)],
                device_id=dev(o), device_id_type=MESH,
            )

    def send(s, fields, far):
        for o, copy in copies(s, fields, far):
            pl.when(exists(o))(copy.start)

    def wait_all(sem, fields, far):
        for cx, cy, cz in itertools.product((1, 2), (1, 2) if far else (0,), (1, 2)):
            if far:
                total = 16 * cy + cx * cy + cy * cz * (1 + cx)
            else:
                total = 16 * cx + 8 * cz + 8 * cx * cz
            match = (sides[0] == cx + 1) & (sides[2] == cz + 1)
            if far:
                match = match & (sides[1] == cy + 1)

            @pl.when(match)
            def _(total=total):
                whole = count.at[pl.ds(0, total * fields)]
                pltpu.make_async_copy(whole, whole, sem).wait()

    def receive(s, fields, far):
        wait_all(rsem.at[s, int(far)], fields, far)

    def sent(s, fields):
        for far in (True, False):
            wait_all(ssem.at[s, int(far)], fields, far)

    def merge(minus, plus):
        return jnp.where(even, pltpu.roll(plus, 127, 1), pltpu.roll(minus, 1, 1))

    def shifted(m, minus, plus):
        m = m + jnp.where(lane < 4, pltpu.roll(minus, 68, 1), 0.0)
        return m + jnp.where((lane >= 60) & (lane < 64), pltpu.roll(plus, 60, 1), 0.0)

    def finish_near(s, f, out):
        m = merge(ZF[s, f, 0], ZF[s, f, 1])
        m = shifted(m, merge(XZ[s, f, 0], XZ[s, f, 1]), merge(XZ[s, f, 2], XZ[s, f, 3]))
        for i in range(32):
            at = (i // 2, pl.ds(8 * (i % 2), 8), slice(None))
            part = jnp.where(ends_z, pltpu.roll(m, 127 - 2 * i, 1), 0.0)
            out[at] = T[(s, f) + at] + part
        for e in (0, 1):
            out[15 * e] = out[15 * e] + XF[s, f, e]

    def from_far(s, f):
        rb = RB.at[s, f]

        def line(k):
            return jnp.broadcast_to(rb[pl.ds(k, 1), :], (8, 128))

        parts = []
        for e in (0, 1):
            m, minus, plus = (merge(line(k + 2 * e), line(k + 2 * e + 1)) for k in (4, 8, 12))
            m = jnp.broadcast_to(shifted(m, minus, plus)[0:1], (16, 128))
            at = 4 * row16 + 2 * (1 - e)
            last = jnp.sum(jnp.where(lane16 == at, m, 0.0), axis=1, keepdims=True)
            first = jnp.sum(jnp.where(lane16 == at + 1, m, 0.0), axis=1, keepdims=True)
            part = YF[s, f, e]
            part = part + jnp.where(row16 == 0, rb[pl.ds(e, 1), :], 0.0)
            part = part + jnp.where(row16 == 15, rb[pl.ds(2 + e, 1), :], 0.0)
            part = part + jnp.where(lane16 == 0, first, 0.0) + jnp.where(lane16 == 127, last, 0.0)
            parts.append(part)
        return parts

    def finish(s, f, out):
        finish_near(s, f, out)
        add_rows(out, from_far(s, f))

    def local_y(v):
        v3 = v.reshape(32, 8, 128)
        slope = my_ref[...].reshape(32, 8, 128) * along_y(v3, facs_ref[0])
        return mass_ref[...] * v + along_y(slope, facs_ref[1]).reshape(16, 16, 128)

    def local_faces(parts, gains):
        both = jnp.concatenate(parts, axis=0).reshape(4, 8, 128)
        slope = gains[1].reshape(4, 8, 128) * along_lanes(both, lanes_ref.at[0])
        total = along_lanes(slope, lanes_ref.at[1])
        slope = gains[0].reshape(4, 8, 128) * along_y(both, facs_ref[0])
        total = (total + along_y(slope, facs_ref[1])).reshape(32, 128)
        return total[:16], total[16:]

    def local(v):
        total = local_y(v)
        slope = along_x(slabs(v), TABLE)
        slope = [mx_ref[i] * slope[i] for i in range(16)]
        total = total + jnp.stack(along_x(slope, TABLE.T))
        slope = mz_ref[...].reshape(256, 128) * along_z(v, mats_ref[0])
        return total + along_z(slope, mats_ref[1]).reshape(16, 16, 128)

    def product(slot, a, b):
        acc[slot] = jnp.sum((a * b).reshape(32, 8, 128), axis=0)

    for ref in (XF, YF, ZF, XZ, RB):
        ref[1:] = jnp.zeros((ITERS,) + ref.shape[1:], jnp.float32)
    acc[...] = jnp.zeros_like(acc)
    Z[0] = jnp.zeros((16, 16, 128), jnp.float32)
    loads[0].wait()
    prepare(0, 0, src_ref[...], True)
    for load in loads[1:]:
        load.wait()
    diag = mass_ref[...] + jnp.stack(along_x_plain(slabs(mx_ref[...]), (TABLE * TABLE).T))
    Y[...] = along_y(my_ref[...].reshape(32, 8, 128), facs_ref[2]).reshape(16, 16, 128)
    diag = diag + Y[...]
    diag = diag + along_z(mz_ref[...], mats_ref[2]).reshape(16, 16, 128)
    prepare(0, 1, diag, True)
    pl.semaphore_wait(barrier, n_near + (plane - 1) + (ring - 1))
    send(0, 2, True)
    send(0, 2, False)
    both = [jnp.concatenate(rows(ref), axis=0) for ref in (mx_ref, mz_ref)]
    FC[0], FC[1] = both
    FC[2] = jnp.concatenate([a + b for a, b in zip(rows(mass_ref), rows(Y))], axis=0)
    def far_faces(s, smooth, change):
        more = local_faces(smooth, (FC[0], FC[1]))
        own = [FC[2, pl.ds(16 * e, 16)] * change[e] for e in (0, 1)]
        prepare_faces(s, [a + b + c for a, b, c in zip(rows(Y), more, own)])
        send(s, 1, True)

    receive(0, 2, False)
    finish_near(0, 0, Z.at[1])
    finish_near(0, 1, jac)
    diag_rows = rows(jac)
    jac[...] = 1.0 / jac[...]
    V[0] = jac[...] * Z[1]
    Y[...] = local_y(V[0])
    receive(0, 2, True)
    d_base = from_far(0, 0)
    jac_rows = [1.0 / (a + b) for a, b in zip(diag_rows, from_far(0, 1))]
    smooth = [a * (b + c) for a, b, c in zip(jac_rows, rows(Z.at[1]), d_base)]
    far_faces(1, smooth, [a - b for a, b in zip(smooth, rows(V.at[0]))])
    add_rows(Z.at[1], d_base)
    set_rows(jac, jac_rows)
    set_rows(V.at[0], smooth)

    last = ITERS - 1
    for j in range(last):
        s = j + 1
        L[j] = local(V[j])
        prepare(s, 0, L[j], False)
        send(s, 1, False)
        for i in range(j + 1):
            product(4 * j + i, L[j], V[i])
        product(16 + j, src_ref[...], V[j])
        receive(s, 1, False)
        finish_near(s, 0, A.at[j])
        gain = (1.0 if j == 0 else 2.0) / HALF
        z = gain * (A[j] - CENTRE * Z[j + 1]) - (0.0 if j == 0 else 1.0) * Z[j]
        Z[j + 2] = z
        V[j + 1] = jac[...] * z
        if j < last - 1:
            Y[...] = local_y(V[j + 1])
        else:
            L[last] = local(V[last])
            for i in range(ITERS):
                product(4 * last + i, L[i], V[last])
            product(16 + last, src_ref[...], V[last])
        receive(s, 1, True)
        d_image = from_far(s, 0)
        d_base = [gain * d for d in d_image]
        d_smooth = [a * b for a, b in zip(rows(jac), d_base)]
        if j < last - 1:
            far_faces(s + 1, [a + b for a, b in zip(rows(V.at[j + 1]), d_smooth)], d_smooth)
        else:
            more = local_faces(d_smooth, (FC[0], FC[1]))
            own = [FC[2, pl.ds(16 * e, 16)] * d_smooth[e] + more[e] for e in (0, 1)]

            def add_product(slot, parts):
                part = sum((a * b).reshape(2, 8, 128)[h] for a, b in zip(parts, d_smooth) for h in (0, 1))
                acc[slot] = acc[slot] + part

            for i in range(last):
                add_product(4 * last + i, rows(L.at[i]))
            add_product(5 * last, [2.0 * a + b for a, b in zip(rows(L.at[last]), own)])
            add_product(16 + last, rows(src_ref))
        add_rows(A.at[j], d_image)
        add_rows(Z.at[j + 2], d_base)
        add_rows(V.at[j + 1], d_smooth)

    sums = jnp.sum(jnp.sum(acc[...], axis=1), axis=1, keepdims=True)
    pick = lax.broadcasted_iota(jnp.int32, (24, 128), 0) == lax.broadcasted_iota(jnp.int32, (24, 128), 1)

    def share(row, buf, me, group, n, ss, rs, values):
        row[...] = values
        buf[me] = values

        for k in far_first(n):
            pltpu.make_async_remote_copy(
                src_ref=row, dst_ref=buf.at[me], send_sem=ss, recv_sem=rs,
                device_id=group(k), device_id_type=MESH,
            ).start()
        peers = buf.at[pl.ds(0, n - 1)]
        return lambda: pltpu.make_async_copy(peers, peers, rs).wait(), lambda: pltpu.make_async_copy(peers, peers, ss).wait()

    values = jnp.sum(jnp.where(pick, sums, 0.0), axis=0, keepdims=True)
    arrive_a, left_a = share(row_a, buf_a, my_a, dev_a, plane, ssem_a, rsem_a, values)
    prepare(ITERS, 0, local(V[last]), True)
    send(ITERS, 1, True)
    send(ITERS, 1, False)
    arrive_a()
    values = jnp.sum(buf_a[...], axis=0)
    arrive_b, left_b = share(row_b, buf_b, my_b, dev_b, ring, ssem_b, rsem_b, values)
    receive(ITERS, 1, False)
    receive(ITERS, 1, True)
    finish(ITERS, 0, A.at[last])
    sent(0, 2)

    def settle(s, c):
        sent(s, 1)
        return c

    lax.fori_loop(1, ITERS + 1, settle, 0)
    left_a()
    arrive_b()
    values = jnp.broadcast_to(jnp.sum(buf_b[...], axis=0), (8, 128))

    def value(k):
        return jnp.sum(jnp.where(lane == k, values, 0.0), axis=1, keepdims=True)

    H = [[value(4 * max(i, j) + min(i, j)) for j in range(ITERS)] for i in range(ITERS)]
    g = [value(16 + i) for i in range(ITERS)]
    inverse = []
    for k in range(ITERS):
        inv = 1.0 / H[k][k]
        inverse.append(inv)
        for i in range(k + 1, ITERS):
            f = H[i][k] * inv
            for j in range(k + 1, ITERS):
                H[i][j] = H[i][j] - f * H[k][j]
            g[i] = g[i] - f * g[k]
    y = [None] * ITERS
    for k in reversed(range(ITERS)):
        s = g[k]
        for j in range(k + 1, ITERS):
            s = s - H[k][j] * y[j]
        y[k] = s * inverse[k]

    wide = [jnp.broadcast_to(c, (8, 128))[None] for c in y]
    total = wide[0] * V[0].reshape(32, 8, 128)
    rest = Z[1].reshape(32, 8, 128) - wide[0] * A[0].reshape(32, 8, 128)
    for j in range(1, ITERS):
        total = total + wide[j] * V[j].reshape(32, 8, 128)
        rest = rest - wide[j] * A[j].reshape(32, 8, 128)
    out_ref[0] = total.reshape(16, 16, 128)
    out_ref[1] = rest.reshape(16, 16, 128)

    left_b()


def solution(mesh):
    dims = tuple(mesh.shape[a] for a in AXES)
    xwidth = min(4, dims[1] // 2)
    plane, ring = dims[0] * xwidth, dims[1] // xwidth * dims[2]
    steps = ITERS + 1
    f32 = jnp.float32
    block = (16, 16, 128)
    vmem = pl.BlockSpec(memory_space=pltpu.VMEM)
    dma = pltpu.SemaphoreType.DMA

    def body(*args):
        def run(*refs):
            kernel(dims, xwidth, *refs)

        mats, facs, lanes = constants()
        both = pl.pallas_call(
            run,
            out_shape=pltpu.VMEM((2,) + block, f32),
            in_specs=[pl.BlockSpec(memory_space=pltpu.HBM)] * 8,
            out_specs=vmem,
            scratch_shapes=[
                *[pltpu.VMEM(block, f32)] * 5,
                pltpu.VMEM(mats.shape, f32),
                pltpu.VMEM(facs.shape, f32),
                pltpu.VMEM(lanes.shape, f32),
                pltpu.VMEM(block, f32),
                pltpu.VMEM((steps, 2) + block, f32),
                pltpu.VMEM(block, f32),
                pltpu.VMEM((ITERS,) + block, f32),
                pltpu.VMEM((ITERS,) + block, f32),
                pltpu.VMEM((ITERS + 1,) + block, f32),
                pltpu.VMEM((ITERS,) + block, f32),
                pltpu.VMEM((steps, 2, 2, 16, 128), f32),
                pltpu.VMEM((steps, 2, 8, 128), f32),
                pltpu.VMEM((steps, 2, 8, 128), f32),
                pltpu.VMEM((3, 32, 128), f32),
                pltpu.VMEM((steps, 2, 2, 16, 128), f32),
                pltpu.VMEM((steps, 2, 2, 16, 128), f32),
                pltpu.VMEM((steps, 2, 2, 8, 128), f32),
                pltpu.VMEM((steps, 2, 4, 8, 128), f32),
                pltpu.VMEM((steps, 2, 16, 128), f32),
                pltpu.VMEM((24, 8, 128), f32),
                pltpu.VMEM((256, 128), f32),
                pltpu.VMEM((1, 128), f32),
                pltpu.VMEM((1, 128), f32),
                pltpu.VMEM((plane, 1, 128), f32),
                pltpu.VMEM((ring, 1, 128), f32),
                dma((steps, 2)),
                dma((steps, 2)),
                dma,
                dma,
                dma,
                dma,
                dma((8,)),
            ],
            compiler_params=pltpu.CompilerParams(
                collective_id=0, has_side_effects=True, vmem_limit_bytes=32 * 1024 * 1024
            ),
        )(*(pltpu.with_memory_space_constraint(a, pltpu.HBM) for a in (*args, jnp.asarray(mats), jnp.asarray(facs), jnp.asarray(lanes))))
        return both[0], both[1]

    spec = P(*AXES)
    return jax.shard_map(
        body, mesh=mesh, in_specs=(spec,) * 5, out_specs=(spec,) * 2, check_vma=False
    )
```
